128 devices in a mesh: gx: 4 (over z), gy: 4 (over y), gz: 8 (over x, core).
Axes of the slice: x: 4, y: 4, z: 4, core: 2. Of those that a mesh axis runs over, the one named last changes fastest.
Arguments:
- rhs: float32 [64, 256, 1024], P('gx', 'gy', 'gz'), may hold values from -8 to 8
- kappa: float32 [64, 256, 1024], P('gx', 'gy', 'gz'), may hold values from 0.09 to 10.1
- sigma: float32 [64, 256, 1024], P('gx', 'gy', 'gz'), may hold values from 0.0005 to 0.01
Outputs:
- correction: float32 [64, 256, 1024], P('gx', 'gy', 'gz')
The draws below stay inside these ranges and needn't reach their ends.
All inputs are finite; a program needn't handle non-finite values.
Results may differ from the reference program's by a relative error of at most 0.0001.
Values sent between devices are 32-bit elements; how exact they have to be, the bound alone decides.
A program may use at most 256 MiB of HBM per device.

```python
import math
import jax
import jax.numpy as jnp

LEVELS = 4
SWEEPS = 6
BOTTOM_SWEEPS = 8
NX = 64
NY = 256
NZ = 1024


def smooth_bump(count_a, count_b, count_c):
    first = jnp.sin(math.pi * (jnp.arange(count_a, dtype=jnp.float32) + 0.5) / count_a)
    second = jnp.sin(math.pi * (jnp.arange(count_b, dtype=jnp.float32) + 0.5) / count_b)
    third = jnp.sin(math.pi * (jnp.arange(count_c, dtype=jnp.float32) + 0.5) / count_c)
    return first[:, None, None] * second[None, :, None] * third[None, None, :]


def wave_field(phases, count_a, count_b, count_c):
    first = jnp.cos(2.0 * math.pi * (jnp.arange(count_a, dtype=jnp.float32) + 0.5) / count_a + phases[0])
    second = jnp.cos(2.0 * math.pi * (jnp.arange(count_b, dtype=jnp.float32) + 0.5) / count_b + phases[1])
    third = jnp.cos(2.0 * math.pi * (jnp.arange(count_c, dtype=jnp.float32) + 0.5) / count_c + phases[2])
    return (first[:, None, None] + second[None, :, None] + third[None, None, :]) / 3.0


def draw_rhs(key, part):
    key = jax.random.fold_in(key, 11)
    bump = smooth_bump(NX, NY, NZ)
    rough = jnp.clip(jax.random.normal(key, (NX, NY, NZ), jnp.float32), -4.5, 4.5)
    field = rough + 3.0 * bump
    return field.astype(jnp.float32)


def draw_kappa(key, part):
    key = jax.random.fold_in(key, 23)
    phase_key, rough_key = jax.random.split(key)
    phases = jax.random.uniform(phase_key, (3,), jnp.float32, 0.0, 2.0 * math.pi)
    smooth = wave_field(phases, NX, NY, NZ)
    rough = jnp.exp(jax.random.uniform(rough_key, (NX, NY, NZ), jnp.float32, -1.15, 1.15))
    field = rough * jnp.exp(1.15 * smooth)
    return field.astype(jnp.float32)


def shard_levels(stream_key, extent, cuts, low, top_value):
    def one(position, parts):
        heights = jax.random.uniform(jax.random.fold_in(jax.random.fold_in(stream_key, 6), position), (parts,), jnp.float32, low / len(cuts), top_value / len(cuts))
        return jnp.repeat(jnp.exp(heights), extent[position] // parts).reshape((-1,) + (1,) * (len(extent) - position - 1))

    gain = one(*cuts[0])
    for cut in cuts[1:]:
        gain = gain * one(*cut)
    return gain


def setup_inputs(seed: int = 0) -> dict:
    arg_keys = jax.random.split(jax.random.key(seed), 4)
    rhs = draw_rhs(jax.random.fold_in(arg_keys[3], 71), 0)
    kappa = draw_kappa(jax.random.fold_in(arg_keys[3], 71), 0)
    sigma = jnp.clip(jnp.exp(math.log(0.01) - 2.9957322 * jax.random.uniform(arg_keys[2], (NX, NY, NZ), jnp.float32) ** shard_levels(arg_keys[2], (NX, NY, NZ), ((0, 4), (1, 4), (2, 8)), -0.2, 0.2)), 0.0005, 0.01)
    return {"rhs": rhs, "kappa": kappa, "sigma": sigma}


SHIFTS = ((1, 0, 0), (-1, 0, 0), (0, 1, 0), (0, -1, 0), (0, 0, 1), (0, 0, -1))
MIDDLE_STENCIL = (0, 0, 0)


def cheb(count):
    return [1.0 / (1.125 + 0.875 * math.cos(math.pi * (2 * t + 1) / (2 * count))) for t in range(count)]


def slice_window(field, exterior_region, interior_region, stencil_shift):
    return field[exterior_region - interior_region + stencil_shift[0]: field.shape[0] - exterior_region + interior_region + stencil_shift[0],
                 exterior_region - interior_region + stencil_shift[1]: field.shape[1] - exterior_region + interior_region + stencil_shift[1],
                 exterior_region - interior_region + stencil_shift[2]: field.shape[2] - exterior_region + interior_region + stencil_shift[2]]


def apply_stencil_operator(value_border, kappa_border, reaction_term, cell_scale, exterior_region, interior_region):
    middle_point = slice_window(value_border, exterior_region, interior_region, MIDDLE_STENCIL)
    kcentre = slice_window(kappa_border, exterior_region, interior_region, MIDDLE_STENCIL)
    face_flux = jnp.zeros_like(middle_point)
    for stencil_shift in SHIFTS:
        face_weight = 0.5 * (kcentre + slice_window(kappa_border, exterior_region, interior_region, stencil_shift))
        face_flux = face_flux + face_weight * (middle_point - slice_window(value_border, exterior_region, interior_region, stencil_shift))
    return cell_scale * face_flux + reaction_term * middle_point


def diagonal(kappa_border, reaction_term, cell_scale, exterior_region, interior_region):
    kcentre = slice_window(kappa_border, exterior_region, interior_region, MIDDLE_STENCIL)
    weight = jnp.zeros_like(kcentre)
    for stencil_shift in SHIFTS:
        weight = weight + 0.5 * (kcentre + slice_window(kappa_border, exterior_region, interior_region, stencil_shift))
    return cell_scale * weight + reaction_term


def restrict(field):
    n0, n1, n2 = field.shape
    return field.reshape(n0 // 2, 2, n1 // 2, 2, n2 // 2, 2).mean(axis=(1, 3, 5))


def prolong(field):
    return jnp.repeat(jnp.repeat(jnp.repeat(field, 2, axis=0), 2, axis=1), 2, axis=2)


def pad_zero(field):
    return jnp.pad(field, 1)


def relax(guess, rhs, kappa_border, reaction_term, diag, cell_scale, weights):
    for weight in weights:
        if guess is None:
            guess = weight * rhs / diag
        else:
            image = apply_stencil_operator(pad_zero(guess), kappa_border, reaction_term, cell_scale, 1, 0)
            guess = guess + weight * (rhs - image) / diag
    return guess


def reference(rhs, kappa, sigma):
    rhs_now, coef, reaction_term, cell_scale = rhs, kappa, sigma, 1.0
    saved = []
    for level in range(LEVELS):
        kappa_border = pad_zero(coef)
        diag = diagonal(kappa_border, reaction_term, cell_scale, 1, 0)
        guess = relax(None, rhs_now, kappa_border, reaction_term, diag, cell_scale, cheb(SWEEPS))
        residue = rhs_now - apply_stencil_operator(pad_zero(guess), kappa_border, reaction_term, cell_scale, 1, 0)
        saved.append((guess, rhs_now, kappa_border, reaction_term, diag, cell_scale))
        rhs_now = restrict(residue)
        coef = restrict(coef)
        reaction_term = restrict(reaction_term)
        cell_scale = cell_scale * 0.25
    kappa_border = pad_zero(coef)
    diag = diagonal(kappa_border, reaction_term, cell_scale, 1, 0)
    result = relax(None, rhs_now, kappa_border, reaction_term, diag, cell_scale, cheb(BOTTOM_SWEEPS))
    for guess, level_rhs, kappa_border, reaction_term, diag, cell_scale in reversed(saved):
        result = relax(guess + prolong(result), level_rhs, kappa_border, reaction_term, diag, cell_scale, cheb(SWEEPS))
    return result
```

```python
from functools import partial
import math

import jax
import jax.numpy as jnp
from jax import lax
from jax.experimental import pallas as pl
from jax.experimental.pallas import tpu as pltpu
from jax.sharding import PartitionSpec as P

LEVELS = 4
SWEEPS = 6
BOTTOM_SWEEPS = 8
MESH = pl.DeviceIdType.MESH
F32 = jnp.float32
COPIES = 256


def cheb(count):
    return [
        1.0 / (1.125 + 0.875 * math.cos(math.pi * (2 * t + 1) / (2 * count))) for t in range(count)
    ]


def lane(rows):
    return lax.broadcasted_iota(jnp.int32, (rows, 128), 1)


def turn(value, shift):
    shift = shift % 128
    return value if shift == 0 else pltpu.roll(value, shift, 1)


def product(value, matrix):
    return jnp.dot(value, matrix, precision=lax.Precision.HIGHEST, preferred_element_type=F32)


def halving(fine0, coarse0, count):
    i = lax.broadcasted_iota(jnp.int32, (128, 128), 0)
    j = lax.broadcasted_iota(jnp.int32, (128, 128), 1)
    offset = (i - fine0) - 2 * (j - coarse0)
    good = ((offset == 0) | (offset == 1)) & (j >= coarse0) & (j < coarse0 + count)
    return jnp.where(good, 0.125, 0.0).astype(F32)


def doubling(coarse0, fine0, low, high):
    i = lax.broadcasted_iota(jnp.int32, (128, 128), 0)
    j = lax.broadcasted_iota(jnp.int32, (128, 128), 1)
    offset = (j - fine0) - 2 * (i - coarse0)
    good = ((offset == 0) | (offset == 1)) & (j >= low) & (j < high)
    return jnp.where(good, 1.0, 0.0).astype(F32)


class Links:
    def __init__(self, send, recv):
        self.send, self.recv, self.used = send, recv, 0

    def copy(self, src, dst, target, send_ok=None, recv_ok=None):
        k = self.used
        self.used += 1
        made = pltpu.make_async_remote_copy(
            src_ref=src,
            dst_ref=dst,
            send_sem=self.send.at[k],
            recv_sem=self.recv.at[k],
            device_id=target,
            device_id_type=MESH,
        )
        return made, send_ok, recv_ok


def given(flag, action):
    if flag is None:
        action()
    else:
        pl.when(flag)(action)


def start(copies):
    for made, send_ok, _ in copies:
        given(send_ok, made.start)


def wait(copies):
    for made, _, recv_ok in copies:
        given(recv_ok, made.wait_recv)
    for made, send_ok, _ in copies:
        given(send_ok, made.wait_send)


def both(a, b):
    if a is None:
        return b
    return a if b is None else a & b


class Level:
    def __init__(self, tiles, row0, rows, scale, closed=False):
        self.tiles, self.row0, self.rows, self.scale, self.closed = tiles, row0, rows, scale, closed

    def window(self, shift=0):
        return pl.ds(self.row0 + shift, self.rows)

    def beside(self, values):
        n = lane(self.rows)
        left = [turn(v, 1) for v in values]
        right = [turn(v, -1) for v in values]
        if self.tiles == 2:
            left = [jnp.where(n == 0, left[1 - t], left[t]) for t in range(2)]
            right = [jnp.where(n == 127, right[1 - t], right[t]) for t in range(2)]
        return left, right

    def near(self, ref, p, tiles):
        mid = [ref[t, p, self.window(), :] for t in range(self.tiles)]
        left, right = self.beside(mid)
        return mid, [
            (
                ref[t, p + 1, self.window(), :],
                ref[t, p - 1, self.window(), :],
                ref[t, p, self.window(1), :],
                ref[t, p, self.window(-1), :],
                left[t],
                right[t],
            )
            for t in range(tiles)
        ]

    def coefficients(self, kappa, sigma, coef, low, high, finish):
        n = lane(self.rows)

        def body(p, carry):
            mid, around = self.near(kappa, p, self.tiles)
            for t in range(self.tiles):
                k, near = mid[t], list(around[t])
                if self.closed:
                    near[4] = jnp.where(n == 0, 0.0, near[4])
                    near[5] = jnp.where(n == 127, 0.0, near[5])
                face = [(0.5 * self.scale) * (k + j) for j in near]
                diag = face[0] + face[1] + face[2] + face[3] + face[4] + face[5]
                diag = diag + sigma[t, p, self.window(), :]
                inverse = jnp.where(k > 0.0, 1.0 / diag, 0.0)
                if self.closed:
                    face[4] = jnp.where(n == 0, 0.0, face[4])
                    face[5] = jnp.where(n == 127, 0.0, face[5])
                for j in range(6):
                    coef[j, t, p, self.window(), :] = face[j] * inverse
                finish(t, p, diag, inverse)
            return carry

        lax.fori_loop(low, high, body, 0)

    def defect(self, x, rhs, coef, p, tiles):
        mid, around = self.near(x, p, tiles)
        out = []
        for t in range(tiles):
            total = rhs[t, p, self.window(), :] - mid[t]
            for j in range(6):
                total = total + coef[j, t, p, self.window(), :] * around[t][j]
            out.append(total)
        return mid, out

    def sweep(self, src, dst, rhs, coef, weight, low, high):
        def body(p, carry):
            mid, out = self.defect(src, rhs, coef, p, self.tiles)
            for t in range(self.tiles):
                dst[t, p, self.window(), :] = mid[t] + weight * out[t]
            return carry

        lax.fori_loop(low, high, body, 0)

    def residual(self, x, rhs, coef, diag, dst, low, high):
        def body(p, carry):
            _, out = self.defect(x, rhs, coef, p, 1)
            dst[0, p, self.window(), :] = diag[0, p, self.window(), :] * out[0]
            return carry

        lax.fori_loop(low, high, body, 0)


def restrict(load, planes, matrix, store):
    sums = [
        load(2 * i, 0) + load(2 * i, 1) + load(2 * i + 1, 0) + load(2 * i + 1, 1)
        for i in range(planes)
    ]
    rows = sums[0].shape[0]
    out = product(jnp.concatenate(sums, axis=0), matrix)
    for i in range(planes):
        store(i, out[i * rows : (i + 1) * rows, :])


def kernel(rhs, kappa, sigma, out, s):
    gx, gy, gz = lax.axis_index("gx"), lax.axis_index("gy"), lax.axis_index("gz")
    nx, ny, nz = 4, 4, 8
    links = Links(s["send"], s["recv"])
    has = {
        ("x", 1): gx < nx - 1,
        ("x", -1): gx > 0,
        ("y", 1): gy < ny - 1,
        ("y", -1): gy > 0,
        ("z", 1): gz < nz - 1,
        ("z", -1): gz > 0,
        ("x", 0): None,
        ("y", 0): None,
    }

    def clear(ref, *index):
        part = ref.at[index] if index else ref
        part[...] = jnp.zeros(part.shape, F32)

    def clear_edges(ref, planes, rows):
        total = ref.shape[1]
        pl.when(gx == 0)(lambda: clear(ref, 0, pl.ds(0, planes[0])))
        pl.when(gx == nx - 1)(lambda: clear(ref, 0, pl.ds(planes[1], total - planes[1])))
        pl.when(gy == 0)(lambda: clear(ref, 0, slice(None), pl.ds(rows[0], rows[1])))
        pl.when(gy == ny - 1)(lambda: clear(ref, 0, slice(None), pl.ds(rows[2], rows[1])))

    for name in ("K0", "S0", "B0", "N0"):
        clear_edges(s[name], (7, 23), (8, 8, 80))
    for name in ("K1", "S1", "B1", "N1", "E1"):
        clear_edges(s[name], (8, 16), (8, 8, 48))
    for name in ("K2", "S2", "B2", "N2"):
        pl.when(gy == 0)(lambda ref=s[name]: clear(ref, 0, slice(None), pl.ds(8, 16)))
        pl.when(gy == ny - 1)(lambda ref=s[name]: clear(ref, 0, slice(None), pl.ds(40, 16)))
    for name in ("K2", "XA2", "XB2"):
        clear(s[name], 0, 0)
        clear(s[name], 0, 17)
    for name, planes, rows in (("3", 8, 32), ("4", 4, 16)):
        for field in ("K", "XA", "XB"):
            ref = s[field + name]
            clear(ref, 0, 0)
            clear(ref, 0, planes + 1)
            clear(ref, 0, slice(None), pl.ds(0, 8))
            clear(ref, 0, slice(None), pl.ds(8 + rows, 8))
    for name in ("G0", "GN0"):
        clear(s[name])

    @pl.when((gz == 0) | (gz == nz - 1))
    def _():
        for name in ("Z0", "ZN0", "Z1", "Z2"):
            clear(s[name])

    barrier = pltpu.get_barrier_semaphore()
    plane_mates = [
        (lax.rem(gx + i, nx), lax.rem(gy + j, ny), gz)
        for i in range(nx)
        for j in range(ny)
        if i or j
    ]
    line_mates = [(gx, gy, lax.rem(gz + i, nz)) for i in range(1, nz)]
    for mate in plane_mates + line_mates:
        pl.semaphore_signal(barrier, inc=1, device_id=mate, device_id_type=MESH)
    pl.semaphore_wait(barrier, len(plane_mates + line_mates))

    around = [(dx, dy) for dx in (1, -1, 0) for dy in (0, 1, -1) if dx or dy]

    def neighbours(make):
        copies = []
        for dx, dy in around:
            src, dst = make(dx, dy)
            copies.append(
                links.copy(
                    src,
                    dst,
                    (gx + dx, gy + dy, gz),
                    both(has["x", dx], has["y", dy]),
                    both(has["x", -dx], has["y", -dy]),
                )
            )
        return copies

    def sides(src, slots):
        return [
            links.copy(src, slots.at[0], (gx, gy, gz + 1), has["z", 1], has["z", -1]),
            links.copy(src, slots.at[1], (gx, gy, gz - 1), has["z", -1], has["z", 1]),
        ]

    def main0(src, first, ref, h):
        def make(dx, dy):
            sp = {1: (first + 16 - h, h), -1: (first, h), 0: (first, 16)}[dx]
            dp = {1: (7 - h, h), -1: (23, h), 0: (7, 16)}[dx]
            sr = {1: (56, 8), -1: (0, 8), 0: (0, 64)}[dy]
            dr = {1: (8, 8), -1: (80, 8), 0: (16, 64)}[dy]
            base = 0 if src is not ref else 16
            source = src.at[pl.ds(*sp), pl.ds(base + sr[0], sr[1])] if base == 0 else src.at[
                0, pl.ds(*sp), pl.ds(base + sr[0], sr[1])
            ]
            return source, ref.at[0, pl.ds(*dp), pl.ds(*dr)]

        return neighbours(make)

    inner = [
        pltpu.make_async_copy(src, s[name].at[0, pl.ds(7, 16), pl.ds(16, 64)], s["local"].at[k])
        for k, (src, name) in enumerate(((kappa, "K0"), (sigma, "S0"), (rhs, "B0")))
    ]
    for made in inner:
        made.start()
    mains = main0(kappa, 0, s["K0"], 7) + main0(sigma, 0, s["S0"], 6) + main0(rhs, 0, s["B0"], 6)
    start(mains)
    for made in inner:
        made.wait()

    def pack0(load, dst):
        n = lane(64)
        for g in range(2):
            total = jnp.zeros((64, 128), F32)
            for q in range(8):
                moved = turn(load(8 * g + q), 16 * q + 8)
                total = jnp.where((n >= 16 * q) & (n < 16 * q + 16), moved, total)
            dst[g, :, :] = total

    for a, name in enumerate(("K0", "S0", "B0")):
        pack0(lambda i, ref=s[name]: ref[0, 7 + i, 16:80, :], s["P0"].at[a])
    side0 = sides(s["P0"], s["Z0"])
    start(side0)

    to1 = halving(0, 32, 64)
    to2 = halving(32, 48, 32)
    to3 = halving(48, 16 * gz, 16)
    to4 = halving(0, 0, 64)
    own2 = pl.ds(1 + 4 * gx, 4)
    own3 = pl.ds(1 + 2 * gx, 2)
    row3 = pl.ds(pl.multiple_of(8 + 8 * gy, 8), 8)

    def down1(src, first, row, dst):
        def store(i, v):
            dst[0, 8 + i, 16:48, :] = v

        restrict(lambda i, o: src[0, first + i, pl.ds(row + o, 32, stride=2), :], 8, to1, store)

    def down2(src, dst):
        def store(i, v):
            dst[0, 1 + 4 * gx + i, 24:40, :] = v

        restrict(lambda i, o: src[0, 8 + i, pl.ds(16 + o, 16, stride=2), :], 4, to2, store)

    def down3(src, use):
        def store(i, v):
            s["Z3"][use, gz, i, :, :] = v

        restrict(
            lambda i, o: src[0, 1 + 4 * gx + i, pl.ds(24 + o, 8, stride=2), :], 2, to3, store
        )

    def down4(src, dst):
        def store(i, v):
            dst[0, 1 + i, 8:24, :] = v

        restrict(lambda i, o: src[0, 1 + i, pl.ds(8 + o, 16, stride=2), :], 4, to4, store)

    def side1(ref, use):
        n = lane(32)
        total = jnp.zeros((32, 128), F32)
        for q in range(8):
            v = ref[0, 8 + q, 16:48, :]
            v = turn(v + turn(v, 64), 16 * q - 24)
            total = jnp.where((n >= 16 * q) & (n < 16 * q + 16), v, total)
        s["P1"][use, :, :] = total
        return sides(s["P1"].at[use], s["Z1"].at[use])

    def merge1(ref, use):
        n = lane(32)
        ghosts = jnp.where((n % 16) < 8, s["Z1"][use, 0], s["Z1"][use, 1])
        for q in range(8):
            low = turn(ghosts, 24 - 16 * q)
            high = turn(ghosts, 24 - 16 * q + 64)
            v = ref[0, 8 + q, 16:48, :]
            v = jnp.where((n >= 24) & (n < 32), low, v)
            ref[0, 8 + q, 16:48, :] = jnp.where((n >= 96) & (n < 104), high, v)

    def main1(ref, h):
        def make(dx, dy):
            sp = {1: (16 - h, h), -1: (8, h), 0: (8, 8)}[dx]
            dp = {1: (8 - h, h), -1: (16, h), 0: (8, 8)}[dx]
            sr = {1: (40, 8), -1: (16, 8), 0: (16, 32)}[dy]
            dr = {1: (8, 8), -1: (48, 8), 0: (16, 32)}[dy]
            return ref.at[0, pl.ds(*sp), pl.ds(*sr)], ref.at[0, pl.ds(*dp), pl.ds(*dr)]

        return neighbours(make)

    def side2(ref, use):
        return sides(ref.at[0, own2, pl.ds(24, 16)], s["Z2"].at[use])

    def merge2(ref, use):
        for i in range(4):
            p = 1 + 4 * gx + i
            ref[0, p, 24:40, :] = (
                ref[0, p, 24:40, :]
                + turn(s["Z2"][use, 0, i], -32)
                + turn(s["Z2"][use, 1, i], 32)
            )

    def main2(ref):
        copies = []
        for i in range(nx):
            for dy in (0, 1, -1):
                if i == 0 and dy == 0:
                    continue
                dr = {1: (8, 16), -1: (40, 16), 0: (24, 16)}[dy]
                copies.append(
                    links.copy(
                        ref.at[0, own2, pl.ds(24, 16)],
                        ref.at[0, own2, pl.ds(*dr)],
                        (lax.rem(gx + i, nx), gy + dy, gz),
                        has["y", dy],
                        has["y", -dy],
                    )
                )
        return copies

    def side3(use):
        part = s["Z3"].at[use, gz]
        return [links.copy(part, part, mate) for mate in line_mates]

    def merge3(ref, use):
        for i in range(2):
            total = s["Z3"][use, 0, i]
            for q in range(1, nz):
                total = total + s["Z3"][use, q, i]
            ref[0, 1 + 2 * gx + i, row3, :] = total

    def main3(ref):
        part = ref.at[0, own3, row3]
        return [links.copy(part, part, mate) for mate in plane_mates]

    down1(s["K0"], 7, 16, s["K1"])
    down1(s["S0"], 7, 16, s["S1"])
    sent = side1(s["K1"], 0) + side1(s["S1"], 1)
    start(sent)
    down2(s["K1"], s["K2"])
    down2(s["S1"], s["S2"])
    more = side2(s["K2"], 0) + side2(s["S2"], 1)
    start(more)
    sent = sent + more
    down3(s["K2"], 0)
    down3(s["S2"], 1)
    more = side3(0) + side3(1)
    start(more)
    sent = sent + more

    wait(side0)
    n64 = lane(64)
    for a in range(3):
        for g in range(2):
            s["G0"][a, 1 + g, 8:72, :] = jnp.where(
                (n64 % 16) < 8, s["Z0"][0, a, g], s["Z0"][1, a, g]
            )

    def ghost0(ref):
        def make(dx, dy):
            sg = {1: (2, 1), -1: (1, 1), 0: (1, 2)}[dx]
            dg = {1: (0, 1), -1: (3, 1), 0: (1, 2)}[dx]
            sr = {1: (64, 8), -1: (8, 8), 0: (8, 64)}[dy]
            dr = {1: (0, 8), -1: (72, 8), 0: (8, 64)}[dy]
            every = slice(None)
            return ref.at[every, pl.ds(*sg), pl.ds(*sr)], ref.at[every, pl.ds(*dg), pl.ds(*dr)]

        return neighbours(make)

    def unpack0(src, ref):
        n = lane(80)
        edge = (n < 8) | (n >= 120)

        for g in range(4):
            v = src[g]
            for q in range(8):
                p = 8 * g + q - 1
                if 0 <= p < 30:
                    ref[1, p, 8:88, :] = jnp.where(edge, turn(v, -16 * q - 8), 0.0)

    ghosts = ghost0(s["G0"])
    start(ghosts)

    wait(sent)
    merge1(s["K1"], 0)
    merge1(s["S1"], 1)
    merge2(s["K2"], 0)
    merge2(s["S2"], 1)
    merge3(s["K3"], 0)
    merge3(s["S3"], 1)
    coarse = main1(s["K1"], 7) + main1(s["S1"], 7) + main2(s["K2"]) + main2(s["S2"])
    coarse = coarse + main3(s["K3"]) + main3(s["S3"])
    start(coarse)

    wait(ghosts)
    for a, name in enumerate(("K0", "S0", "B0")):
        unpack0(s["G0"].at[a], s[name])
    wait(mains)

    weights = cheb(SWEEPS)
    level0 = Level(2, 8, 80, 1.0)
    c0, b0, xa0, xb0 = s["C0"], s["B0"], s["S0"], s["XB0"]

    def finish0(t, p, diag, inverse):
        scaled = b0[t, p, 8:88, :] * inverse
        b0[t, p, 8:88, :] = scaled
        xa0[t, p, 8:88, :] = weights[0] * scaled
        if t == 0:
            s["D0"][0, p, :, :] = diag[8:72, :]

    level0.coefficients(s["K0"], s["S0"], c0, 1, 29, finish0)
    x, y = xa0, xb0
    for t in range(1, SWEEPS):
        level0.sweep(x, y, b0, c0, weights[t], 7 - (6 - t), 23 + (6 - t))
        x, y = y, x

    inside0 = Level(2, 16, 64, 1.0)

    def residual0(p, carry):
        _, defect = inside0.defect(x, b0, c0, p, 1)
        s["R0"][0, p, 0:64, :] = s["D0"][0, p, :, :] * defect[0]
        return carry

    lax.fori_loop(7, 23, residual0, 0)
    pre0 = x

    down1(s["R0"], 7, 0, s["B1"])
    round1 = side1(s["B1"], 2)
    start(round1)

    wait(coarse)
    level1 = Level(1, 8, 48, 0.25)
    level2 = Level(1, 8, 48, 0.0625)
    level3 = Level(1, 8, 32, 0.015625, closed=True)
    level4 = Level(1, 8, 16, 0.00390625)
    down4(s["K3"], s["K4"])
    down4(s["S3"], s["S4"])

    def finish(level, name):
        def keep(t, p, diag, inverse):
            s["D" + name][t, p, level.window(), :] = diag
            s["I" + name][t, p, level.window(), :] = inverse

        return keep

    level1.coefficients(s["K1"], s["S1"], s["C1"], 2, 22, finish(level1, "1"))
    wait(round1)
    merge1(s["B1"], 2)
    round1 = main1(s["B1"], 6)
    start(round1)

    pack0(lambda i: pre0[0, 7 + i, 16:80, :], s["PN0"].at[0])
    side_n0 = sides(s["PN0"], s["ZN0"])
    start(side_n0)
    level2.coefficients(s["K2"], s["S2"], s["C2"], 1, 17, finish(level2, "2"))
    level3.coefficients(s["K3"], s["S3"], s["C3"], 1, 9, finish(level3, "3"))
    level4.coefficients(s["K4"], s["S4"], s["C4"], 1, 5, finish(level4, "4"))

    def begin(level, name, low, high):
        def body(p, carry):
            part = (0, p, level.window(), slice(None))
            scaled = s["B" + name][part] * s["I" + name][part]
            s["B" + name][part] = scaled
            s["XA" + name][part] = first_weight(name) * scaled
            return carry

        lax.fori_loop(low, high, body, 0)

    def first_weight(name):
        return cheb(BOTTOM_SWEEPS if name == "4" else SWEEPS)[0]

    wait(round1)
    begin(level1, "1", 2, 22)
    x, y = s["XA1"], s["XB1"]
    for t in range(1, SWEEPS):
        h = 6 - t
        level1.sweep(x, y, s["B1"], s["C1"], weights[t], 8 - h, 16 + h)
        x, y = y, x
    level1.residual(x, s["B1"], s["C1"], s["D1"], y, 8, 16)

    down2(y, s["B2"])
    round2 = side2(s["B2"], 2)
    start(round2)
    n32 = lane(32)
    for i in range(8):
        s["N1"][0, 8 + i, 16:48, :] = jnp.where(
            (n32 >= 32) & (n32 < 96), x[0, 8 + i, 16:48, :], 0.0
        )
    wait(round2)
    merge2(s["B2"], 2)
    round2 = main2(s["B2"])
    start(round2)
    side_n1 = side1(s["N1"], 3)
    start(side_n1)
    wait(round2)
    begin(level2, "2", 1, 17)
    x, y = s["XA2"], s["XB2"]
    for t in range(1, SWEEPS):
        level2.sweep(x, y, s["B2"], s["C2"], weights[t], 1, 17)
        x, y = y, x
    level2.residual(x, s["B2"], s["C2"], s["D2"], s["R2"], 1, 17)

    down3(s["R2"], 2)
    round3 = side3(2)
    start(round3)
    n16 = lane(16)
    for i in range(4):
        p = 1 + 4 * gx + i
        s["N2"][0, p, 24:40, :] = jnp.where((n16 >= 48) & (n16 < 80), x[0, p, 24:40, :], 0.0)
    wait(round3)
    merge3(s["B3"], 2)
    round3 = main3(s["B3"])
    start(round3)

    side_n2 = side2(s["N2"], 3)
    start(side_n2)
    wait(side_n0)
    for g in range(2):
        s["GN0"][0, 1 + g, 8:72, :] = jnp.where(
            (n64 % 16) < 8, s["ZN0"][0, 0, g], s["ZN0"][1, 0, g]
        )
    ghosts = ghost0(s["GN0"])
    wait(side_n1)
    merge1(s["N1"], 3)
    wait(side_n2)
    merge2(s["N2"], 3)
    wait(round3)
    main_n2 = main2(s["N2"])
    start(main_n2)
    main_n1 = main1(s["N1"], 6)
    start(main_n1)
    start(ghosts)
    for i in range(16):
        s["N0"][0, 7 + i, 16:80, :] = pre0[0, 7 + i, 16:80, :]
    main_n0 = main0(s["N0"], 7, s["N0"], 6)
    start(main_n0)

    begin(level3, "3", 1, 9)
    x, y = s["XA3"], s["XB3"]
    for t in range(1, SWEEPS):
        level3.sweep(x, y, s["B3"], s["C3"], weights[t], 1, 9)
        x, y = y, x
    level3.residual(x, s["B3"], s["C3"], s["D3"], s["R3"], 1, 9)
    down4(s["R3"], s["B4"])

    begin(level4, "4", 1, 5)
    u, v = s["XA4"], s["XB4"]
    for weight in cheb(BOTTOM_SWEEPS)[1:]:
        level4.sweep(u, v, s["B4"], s["C4"], weight, 1, 5)
        u, v = v, u

    def spread(rows, planes, matrix, load, dst):
        value = product(jnp.concatenate([load(i) for i in range(planes)], axis=0), matrix)
        for i in range(planes):
            part = value[i * rows : (i + 1) * rows, :]
            dst[i, pl.ds(0, rows, stride=2), :] = part
            dst[i, pl.ds(1, rows, stride=2), :] = part

    fine = s["T"]
    spread(16, 4, doubling(0, 0, 0, 128), lambda i: u[0, 1 + i, 8:24, :], fine)
    for i in range(8):
        y[0, 1 + i, 8:40, :] = x[0, 1 + i, 8:40, :] + fine[i // 2, 0:32, :]
    for t in range(SWEEPS):
        x, y = y, x
        level3.sweep(x, y, s["B3"], s["C3"], weights[t], 1, 9)
    e3 = y

    wait(main_n2)
    rows3 = pl.ds(pl.multiple_of(8 * gy, 8), 24)
    spread(24, 8, doubling(16 * gz, 48, 16, 112), lambda i: e3[0, 1 + i, rows3, :], fine)
    y, x = s["XA2"], s["XB2"]
    for i in range(16):
        y[0, 1 + i, 8:56, :] = s["N2"][0, 1 + i, 8:56, :] + fine[i // 2, 0:48, :]
    for t in range(SWEEPS):
        x, y = y, x
        level2.sweep(x, y, s["B2"], s["C2"], weights[t], 1, 17)
    e2 = y

    wait(main_n1)
    value = product(
        jnp.concatenate([e2[0, 1 + i, 20:44, :] for i in range(16)], axis=0),
        doubling(48, 32, 24, 104),
    )
    fine1 = s["T1"]
    pl.when(gx == 0)(lambda: clear(fine1, pl.ds(0, 4)))
    pl.when(gx == nx - 1)(lambda: clear(fine1, pl.ds(20, 4)))
    for i in range(16):
        part = value[i * 24 : (i + 1) * 24, :]
        fine1[4 + i, pl.ds(0, 24, stride=2), :] = part
        fine1[4 + i, pl.ds(1, 24, stride=2), :] = part
    y, x = s["XA1"], s["XB1"]
    for p in range(-6, 14):
        y[0, 8 + p, 8:56, :] = s["N1"][0, 8 + p, 8:56, :] + fine1[4 + 4 * gx + p // 2, 0:48, :]
    for t in range(SWEEPS):
        x, y = y, x
        h = 5 - t
        level1.sweep(x, y, s["B1"], s["C1"], weights[t], 8 - h, 16 + h)
    for i in range(8):
        s["E1"][0, 8 + i, 16:48, :] = jnp.where(
            (n32 >= 32) & (n32 < 96), y[0, 8 + i, 16:48, :], 0.0
        )
    round1 = side1(s["E1"], 4)
    start(round1)
    wait(ghosts)
    unpack0(s["GN0"].at[0], s["N0"])
    wait(round1)
    merge1(s["E1"], 4)
    round1 = main1(s["E1"], 3)
    start(round1)
    wait(main_n0)
    wait(round1)

    to_main = doubling(32, 0, 0, 128)
    to_side = doubling(32, -128, 0, 8) + doubling(32, 128, 120, 128)
    xa0 = s["S0"]
    for i in range(14):
        e = s["E1"][0, 5 + i, 12:52, :]
        for t, matrix in ((0, to_main), (1, to_side)):
            part = product(e, matrix)
            s["T0"][t, pl.ds(0, 40, stride=2), :] = part
            s["T0"][t, pl.ds(1, 40, stride=2), :] = part
            for o in range(2):
                p = 1 + 2 * i + o
                xa0[t, p, 8:88, :] = s["N0"][t, p, 8:88, :] + s["T0"][t, 0:80, :]
    x, y = s["XB0"], xa0
    for t in range(SWEEPS - 1):
        x, y = y, x
        h = 5 - t
        level0.sweep(x, y, b0, c0, weights[t], 7 - h, 23 + h)

    def last(p, carry):
        mid, defect = inside0.defect(y, b0, c0, p, 1)
        out[p - 7, :, :] = mid[0] + weights[SWEEPS - 1] * defect[0]
        return carry

    lax.fori_loop(7, 23, last, 0)


def scratch():
    shapes = {}
    for name in ("K0", "S0", "B0", "N0", "XB0"):
        shapes[name] = (2, 30, 96, 128)
    shapes["C0"] = (6, 2, 30, 96, 128)
    shapes["D0"], shapes["R0"] = (1, 30, 64, 128), (1, 23, 72, 128)
    shapes["P0"], shapes["Z0"], shapes["G0"] = (3, 2, 64, 128), (2, 3, 2, 64, 128), (3, 4, 80, 128)
    shapes["PN0"], shapes["ZN0"] = (1, 2, 64, 128), (2, 1, 2, 64, 128)
    shapes["GN0"] = (1, 4, 80, 128)
    shapes["T0"] = (2, 88, 128)
    for level, dims in (("1", (24, 64, 128)), ("2", (18, 64, 128)), ("3", (10, 48, 128)), ("4", (6, 32, 128))):
        for name in ("K", "S", "B", "I", "D", "XA", "XB"):
            shapes[name + level] = (1,) + dims
        shapes["C" + level] = (6, 1) + dims
    shapes["N1"] = shapes["E1"] = shapes["K1"]
    shapes["N2"] = shapes["R2"] = shapes["K2"]
    shapes["R3"] = shapes["K3"]
    shapes["P1"], shapes["Z1"] = (5, 32, 128), (5, 2, 32, 128)
    shapes["Z2"] = (4, 2, 4, 16, 128)
    shapes["Z3"] = (3, 8, 2, 8, 128)
    shapes["T"], shapes["T1"] = (8, 56, 128), (24, 56, 128)
    return {
        "send": pltpu.SemaphoreType.DMA((COPIES,)),
        "recv": pltpu.SemaphoreType.DMA((COPIES,)),
        "local": pltpu.SemaphoreType.DMA((3,)),
        **{name: pltpu.VMEM(shape, F32) for name, shape in shapes.items()},
    }


def on_device(rhs, kappa, sigma):
    return pl.pallas_call(
        kernel,
        out_shape=jax.ShapeDtypeStruct(rhs.shape, F32),
        in_specs=[pl.BlockSpec(memory_space=pl.ANY)] * 3,
        out_specs=pl.BlockSpec(memory_space=pltpu.VMEM),
        scratch_shapes=[scratch()],
        compiler_params=pltpu.CompilerParams(
            collective_id=0, has_side_effects=True, vmem_limit_bytes=63 * 2**20
        ),
    )(rhs, kappa, sigma)


def solution(mesh):
    placed = (P("gx", "gy", "gz"), P("gx", "gy", "gz"), P("gx", "gy", "gz"))
    return jax.shard_map(
        on_device, mesh=mesh, in_specs=placed, out_specs=P("gx", "gy", "gz"), check_vma=False
    )
```

```python
from functools import partial
import math

import jax
import jax.numpy as jnp
from jax import lax
from jax.experimental import pallas as pl
from jax.experimental.pallas import tpu as pltpu
from jax.sharding import PartitionSpec as P

LEVELS = 4
SWEEPS = 6
BOTTOM_SWEEPS = 8
MESH = pl.DeviceIdType.MESH
F32 = jnp.float32
COPIES = 256


def cheb(count):
    return [
        1.0 / (1.125 + 0.875 * math.cos(math.pi * (2 * t + 1) / (2 * count))) for t in range(count)
    ]


def lane(rows):
    return lax.broadcasted_iota(jnp.int32, (rows, 128), 1)


def turn(value, shift):
    shift = shift % 128
    return value if shift == 0 else pltpu.roll(value, shift, 1)


def product(value, matrix):
    return jnp.dot(value, matrix, precision=lax.Precision.HIGHEST, preferred_element_type=F32)


def halving(fine0, coarse0, count):
    i = lax.broadcasted_iota(jnp.int32, (128, 128), 0)
    j = lax.broadcasted_iota(jnp.int32, (128, 128), 1)
    offset = (i - fine0) - 2 * (j - coarse0)
    good = ((offset == 0) | (offset == 1)) & (j >= coarse0) & (j < coarse0 + count)
    return jnp.where(good, 0.125, 0.0).astype(F32)


def doubling(coarse0, fine0, low, high):
    i = lax.broadcasted_iota(jnp.int32, (128, 128), 0)
    j = lax.broadcasted_iota(jnp.int32, (128, 128), 1)
    offset = (j - fine0) - 2 * (i - coarse0)
    good = ((offset == 0) | (offset == 1)) & (j >= low) & (j < high)
    return jnp.where(good, 1.0, 0.0).astype(F32)


class Links:
    def __init__(self, send, recv):
        self.send, self.recv, self.used = send, recv, 0

    def copy(self, src, dst, target, send_ok=None, recv_ok=None):
        k = self.used
        self.used += 1
        made = pltpu.make_async_remote_copy(
            src_ref=src,
            dst_ref=dst,
            send_sem=self.send.at[k],
            recv_sem=self.recv.at[k],
            device_id=target,
            device_id_type=MESH,
        )
        return made, send_ok, recv_ok


def given(flag, action):
    if flag is None:
        action()
    else:
        pl.when(flag)(action)


def start(copies):
    for made, send_ok, _ in copies:
        given(send_ok, made.start)


def wait(copies):
    for made, _, recv_ok in copies:
        given(recv_ok, made.wait_recv)
    for made, send_ok, _ in copies:
        given(send_ok, made.wait_send)


def both(a, b):
    if a is None:
        return b
    return a if b is None else a & b


def groups(low, high, size, action):
    whole = (high - low) // size
    if whole == 1:
        action(low, size)
    elif whole:

        def body(i, carry):
            action(low + size * i, size)
            return carry

        lax.fori_loop(0, whole, body, 0)
    rest = (high - low) % size
    if rest:
        action(high - rest, rest)


class Level:
    def __init__(self, tiles, scale, closed=False):
        self.tiles, self.scale, self.closed = tiles, scale, closed

    def beside(self, values):
        n = lane(values[0].shape[0])
        left = [turn(v, 1) for v in values]
        right = [turn(v, -1) for v in values]
        if self.tiles == 2:
            left = [jnp.where(n == 0, left[1 - t], left[t]) for t in range(2)]
            right = [jnp.where(n == 127, right[1 - t], right[t]) for t in range(2)]
        return left, right

    def around(self, ref, p, count, row, rows, tiles):
        win = pl.ds(row, rows)
        mid = [[ref[t, p + i - 1, win, :] for i in range(count + 2)] for t in range(tiles)]
        mid += [[None] + [ref[t, p + i, win, :] for i in range(count)] for t in range(tiles, self.tiles)]
        found = []
        for i in range(count):
            left, right = self.beside([mid[t][i + 1] for t in range(self.tiles)])
            for t in range(tiles):
                near = [
                    mid[t][i + 2],
                    mid[t][i],
                    ref[t, p + i, pl.ds(row + 1, rows), :],
                    ref[t, p + i, pl.ds(row - 1, rows), :],
                    left[t],
                    right[t],
                ]
                found.append((t, p + i, mid[t][i + 1], near))
        return found

    def coefficients(self, kappa, sigma, coef, low, high, size, row, rows, chunk, finish):
        def block(first, count):
            for start_row in range(row, row + rows, chunk):
                win = pl.ds(start_row, chunk)
                n = lane(chunk)
                for t, p, k, near in self.around(kappa, first, count, start_row, chunk, self.tiles):
                    if self.closed:
                        near[4] = jnp.where(n == 0, 0.0, near[4])
                        near[5] = jnp.where(n == 127, 0.0, near[5])
                    face = [(0.5 * self.scale) * (k + j) for j in near]
                    diag = (face[0] + face[1]) + (face[2] + face[3]) + (face[4] + face[5])
                    diag = diag + sigma[t, p, win, :]
                    inverse = jnp.where(k > 0.0, 1.0 / diag, 0.0)
                    if self.closed:
                        face[4] = jnp.where(n == 0, 0.0, face[4])
                        face[5] = jnp.where(n == 127, 0.0, face[5])
                    for j in range(6):
                        coef[j, t, p, win, :] = face[j] * inverse
                    finish(t, p, start_row, chunk, diag, inverse)

        groups(low, high, size, block)

    def defects(self, x, rhs, coef, low, high, size, row, rows, chunk, tiles, use):
        def block(first, count):
            for start_row in range(row, row + rows, chunk):
                win = pl.ds(start_row, chunk)
                found = []
                for t, p, mid, near in self.around(x, first, count, start_row, chunk, tiles):
                    c = [coef[j, t, p, win, :] for j in range(6)]
                    a = (c[0] * near[0] + c[1] * near[1]) + (c[2] * near[2] + c[3] * near[3])
                    b = (rhs[t, p, win, :] - mid) + (c[4] * near[4] + c[5] * near[5])
                    found.append((t, p, mid, a + b))
                for t, p, mid, value in found:
                    use(t, p, start_row, chunk, mid, value)

        groups(low, high, size, block)

    def sweep(self, src, dst, rhs, coef, weight, low, high, size, row, rows, chunk):
        def use(t, p, r, n, mid, value):
            dst[t, p, pl.ds(r, n), :] = mid + weight * value

        self.defects(src, rhs, coef, low, high, size, row, rows, chunk, self.tiles, use)

    def residual(self, x, rhs, coef, diag, dst, low, high, size, row, rows, chunk):
        def use(t, p, r, n, mid, value):
            dst[0, p, pl.ds(r, n), :] = diag[0, p, pl.ds(r, n), :] * value

        self.defects(x, rhs, coef, low, high, size, row, rows, chunk, 1, use)


def restrict(load, planes, matrix, store):
    sums = [
        load(2 * i, 0) + load(2 * i, 1) + load(2 * i + 1, 0) + load(2 * i + 1, 1)
        for i in range(planes)
    ]
    rows = sums[0].shape[0]
    out = product(jnp.concatenate(sums, axis=0), matrix)
    for i in range(planes):
        store(i, out[i * rows : (i + 1) * rows, :])


def kernel(rhs, kappa, sigma, out, s):
    gx, gy, gz = lax.axis_index("gx"), lax.axis_index("gy"), lax.axis_index("gz")
    nx, ny, nz = 4, 4, 8
    links = Links(s["send"], s["recv"])
    has = {
        ("x", 1): gx < nx - 1,
        ("x", -1): gx > 0,
        ("y", 1): gy < ny - 1,
        ("y", -1): gy > 0,
        ("z", 1): gz < nz - 1,
        ("z", -1): gz > 0,
        ("x", 0): None,
        ("y", 0): None,
    }

    def clear(ref, *index):
        part = ref.at[index] if index else ref
        part[...] = jnp.zeros(part.shape, F32)

    def clear_edges(ref, planes, rows):
        total = ref.shape[1]
        pl.when(gx == 0)(lambda: clear(ref, 0, pl.ds(0, planes[0])))
        pl.when(gx == nx - 1)(lambda: clear(ref, 0, pl.ds(planes[1], total - planes[1])))
        pl.when(gy == 0)(lambda: clear(ref, 0, slice(None), pl.ds(rows[0], rows[1])))
        pl.when(gy == ny - 1)(lambda: clear(ref, 0, slice(None), pl.ds(rows[2], rows[1])))

    for name in ("K0", "S0", "B0", "N0"):
        clear_edges(s[name], (7, 23), (8, 8, 80))
    for name in ("K1", "S1", "B1", "N1", "E1"):
        clear_edges(s[name], (8, 16), (8, 8, 48))
    for name in ("K2", "S2", "B2", "N2"):
        pl.when(gy == 0)(lambda ref=s[name]: clear(ref, 0, slice(None), pl.ds(8, 16)))
        pl.when(gy == ny - 1)(lambda ref=s[name]: clear(ref, 0, slice(None), pl.ds(40, 16)))
    for name in ("K2", "XA2", "XB2"):
        clear(s[name], 0, 0)
        clear(s[name], 0, 17)
    for name, planes, rows in (("3", 8, 32), ("4", 4, 16)):
        for field in ("K", "XA", "XB"):
            ref = s[field + name]
            clear(ref, 0, 0)
            clear(ref, 0, planes + 1)
            clear(ref, 0, slice(None), pl.ds(0, 8))
            clear(ref, 0, slice(None), pl.ds(8 + rows, 8))
    for name in ("G0", "GN0"):
        clear(s[name])

    @pl.when((gz == 0) | (gz == nz - 1))
    def _():
        for name in ("Z0", "ZN0", "Z1", "Z2"):
            clear(s[name])

    barrier = pltpu.get_barrier_semaphore()
    plane_mates = [
        (lax.rem(gx + i, nx), lax.rem(gy + j, ny), gz)
        for i in range(nx)
        for j in range(ny)
        if i or j
    ]
    line_mates = [(gx, gy, lax.rem(gz + i, nz)) for i in range(1, nz)]
    for mate in plane_mates + line_mates:
        pl.semaphore_signal(barrier, inc=1, device_id=mate, device_id_type=MESH)
    pl.semaphore_wait(barrier, len(plane_mates + line_mates))

    around = [(dx, dy) for dx in (1, -1, 0) for dy in (0, 1, -1) if dx or dy]

    def neighbours(make):
        copies = []
        for dx, dy in around:
            src, dst = make(dx, dy)
            copies.append(
                links.copy(
                    src,
                    dst,
                    (gx + dx, gy + dy, gz),
                    both(has["x", dx], has["y", dy]),
                    both(has["x", -dx], has["y", -dy]),
                )
            )
        return copies

    def sides(src, slots):
        return [
            links.copy(src, slots.at[0], (gx, gy, gz + 1), has["z", 1], has["z", -1]),
            links.copy(src, slots.at[1], (gx, gy, gz - 1), has["z", -1], has["z", 1]),
        ]

    def main0(src, first, ref, h):
        def make(dx, dy):
            sp = {1: (first + 16 - h, h), -1: (first, h), 0: (first, 16)}[dx]
            dp = {1: (7 - h, h), -1: (23, h), 0: (7, 16)}[dx]
            sr = {1: (56, 8), -1: (0, 8), 0: (0, 64)}[dy]
            dr = {1: (8, 8), -1: (80, 8), 0: (16, 64)}[dy]
            base = 0 if src is not ref else 16
            source = src.at[pl.ds(*sp), pl.ds(base + sr[0], sr[1])] if base == 0 else src.at[
                0, pl.ds(*sp), pl.ds(base + sr[0], sr[1])
            ]
            return source, ref.at[0, pl.ds(*dp), pl.ds(*dr)]

        return neighbours(make)

    inner = [
        pltpu.make_async_copy(src, s[name].at[0, pl.ds(7, 16), pl.ds(16, 64)], s["local"].at[k])
        for k, (src, name) in enumerate(((kappa, "K0"), (sigma, "S0"), (rhs, "B0")))
    ]
    for made in inner:
        made.start()
    mains = main0(kappa, 0, s["K0"], 7) + main0(sigma, 0, s["S0"], 6) + main0(rhs, 0, s["B0"], 6)
    start(mains)
    for made in inner:
        made.wait()

    def pack0(load, dst):
        n = lane(64)
        for g in range(2):
            total = jnp.zeros((64, 128), F32)
            for q in range(8):
                moved = turn(load(8 * g + q), 16 * q + 8)
                total = jnp.where((n >= 16 * q) & (n < 16 * q + 16), moved, total)
            dst[g, :, :] = total

    for a, name in enumerate(("K0", "S0", "B0")):
        pack0(lambda i, ref=s[name]: ref[0, 7 + i, 16:80, :], s["P0"].at[a])
    side0 = sides(s["P0"], s["Z0"])
    start(side0)

    to1 = halving(0, 32, 64)
    to2 = halving(32, 48, 32)
    to3 = halving(48, 16 * gz, 16)
    to4 = halving(0, 0, 64)
    own2 = pl.ds(1 + 4 * gx, 4)
    own3 = pl.ds(1 + 2 * gx, 2)
    row3 = pl.ds(pl.multiple_of(8 + 8 * gy, 8), 8)

    def down1(src, first, row, dst):
        def store(i, v):
            dst[0, 8 + i, 16:48, :] = v

        restrict(lambda i, o: src[0, first + i, pl.ds(row + o, 32, stride=2), :], 8, to1, store)

    def down2(src, dst):
        def store(i, v):
            dst[0, 1 + 4 * gx + i, 24:40, :] = v

        restrict(lambda i, o: src[0, 8 + i, pl.ds(16 + o, 16, stride=2), :], 4, to2, store)

    def down3(src, use):
        def store(i, v):
            s["Z3"][use, gz, i, :, :] = v

        restrict(
            lambda i, o: src[0, 1 + 4 * gx + i, pl.ds(24 + o, 8, stride=2), :], 2, to3, store
        )

    def down4(src, dst):
        def store(i, v):
            dst[0, 1 + i, 8:24, :] = v

        restrict(lambda i, o: src[0, 1 + i, pl.ds(8 + o, 16, stride=2), :], 4, to4, store)

    def side1(ref, use):
        n = lane(32)
        total = jnp.zeros((32, 128), F32)
        for q in range(8):
            v = ref[0, 8 + q, 16:48, :]
            v = turn(v + turn(v, 64), 16 * q - 24)
            total = jnp.where((n >= 16 * q) & (n < 16 * q + 16), v, total)
        s["P1"][use, :, :] = total
        return sides(s["P1"].at[use], s["Z1"].at[use])

    def merge1(ref, use):
        n = lane(32)
        ghosts = jnp.where((n % 16) < 8, s["Z1"][use, 0], s["Z1"][use, 1])
        for q in range(8):
            low = turn(ghosts, 24 - 16 * q)
            high = turn(ghosts, 24 - 16 * q + 64)
            v = ref[0, 8 + q, 16:48, :]
            v = jnp.where((n >= 24) & (n < 32), low, v)
            ref[0, 8 + q, 16:48, :] = jnp.where((n >= 96) & (n < 104), high, v)

    def main1(ref, h):
        def make(dx, dy):
            sp = {1: (16 - h, h), -1: (8, h), 0: (8, 8)}[dx]
            dp = {1: (8 - h, h), -1: (16, h), 0: (8, 8)}[dx]
            sr = {1: (40, 8), -1: (16, 8), 0: (16, 32)}[dy]
            dr = {1: (8, 8), -1: (48, 8), 0: (16, 32)}[dy]
            return ref.at[0, pl.ds(*sp), pl.ds(*sr)], ref.at[0, pl.ds(*dp), pl.ds(*dr)]

        return neighbours(make)

    def side2(ref, use):
        return sides(ref.at[0, own2, pl.ds(24, 16)], s["Z2"].at[use])

    def merge2(ref, use):
        for i in range(4):
            p = 1 + 4 * gx + i
            ref[0, p, 24:40, :] = (
                ref[0, p, 24:40, :]
                + turn(s["Z2"][use, 0, i], -32)
                + turn(s["Z2"][use, 1, i], 32)
            )

    def main2(ref):
        copies = []
        for i in range(nx):
            for dy in (0, 1, -1):
                if i == 0 and dy == 0:
                    continue
                dr = {1: (8, 16), -1: (40, 16), 0: (24, 16)}[dy]
                copies.append(
                    links.copy(
                        ref.at[0, own2, pl.ds(24, 16)],
                        ref.at[0, own2, pl.ds(*dr)],
                        (lax.rem(gx + i, nx), gy + dy, gz),
                        has["y", dy],
                        has["y", -dy],
                    )
                )
        return copies

    def side3(use):
        part = s["Z3"].at[use, gz]
        return [links.copy(part, part, mate) for mate in line_mates]

    def merge3(ref, use):
        for i in range(2):
            total = s["Z3"][use, 0, i]
            for q in range(1, nz):
                total = total + s["Z3"][use, q, i]
            ref[0, 1 + 2 * gx + i, row3, :] = total

    def main3(ref):
        part = ref.at[0, own3, row3]
        return [links.copy(part, part, mate) for mate in plane_mates]

    down1(s["K0"], 7, 16, s["K1"])
    down1(s["S0"], 7, 16, s["S1"])
    sent = side1(s["K1"], 0) + side1(s["S1"], 1)
    start(sent)
    down2(s["K1"], s["K2"])
    down2(s["S1"], s["S2"])
    more = side2(s["K2"], 0) + side2(s["S2"], 1)
    start(more)
    sent = sent + more
    down3(s["K2"], 0)
    down3(s["S2"], 1)
    more = side3(0) + side3(1)
    start(more)
    sent = sent + more

    wait(side0)
    n64 = lane(64)
    for a in range(3):
        for g in range(2):
            s["G0"][a, 1 + g, 8:72, :] = jnp.where(
                (n64 % 16) < 8, s["Z0"][0, a, g], s["Z0"][1, a, g]
            )

    def ghost0(ref):
        def make(dx, dy):
            sg = {1: (2, 1), -1: (1, 1), 0: (1, 2)}[dx]
            dg = {1: (0, 1), -1: (3, 1), 0: (1, 2)}[dx]
            sr = {1: (64, 8), -1: (8, 8), 0: (8, 64)}[dy]
            dr = {1: (0, 8), -1: (72, 8), 0: (8, 64)}[dy]
            every = slice(None)
            return ref.at[every, pl.ds(*sg), pl.ds(*sr)], ref.at[every, pl.ds(*dg), pl.ds(*dr)]

        return neighbours(make)

    def unpack0(src, ref):
        n = lane(80)
        edge = (n < 8) | (n >= 120)

        for g in range(4):
            v = src[g]
            for q in range(8):
                p = 8 * g + q - 1
                if 0 <= p < 30:
                    ref[1, p, 8:88, :] = jnp.where(edge, turn(v, -16 * q - 8), 0.0)

    ghosts = ghost0(s["G0"])
    start(ghosts)

    wait(sent)
    merge1(s["K1"], 0)
    merge1(s["S1"], 1)
    merge2(s["K2"], 0)
    merge2(s["S2"], 1)
    merge3(s["K3"], 0)
    merge3(s["S3"], 1)
    coarse = main1(s["K1"], 7) + main1(s["S1"], 7) + main2(s["K2"]) + main2(s["S2"])
    coarse = coarse + main3(s["K3"]) + main3(s["S3"])
    start(coarse)

    wait(ghosts)
    for a, name in enumerate(("K0", "S0", "B0")):
        unpack0(s["G0"].at[a], s[name])
    wait(mains)

    weights = cheb(SWEEPS)
    level0 = Level(2, 1.0)
    c0, b0, xa0, xb0 = s["C0"], s["B0"], s["S0"], s["XB0"]

    def finish0(t, p, r, n, diag, inverse):
        win = pl.ds(r, n)
        scaled = b0[t, p, win, :] * inverse
        b0[t, p, win, :] = scaled
        xa0[t, p, win, :] = weights[0] * scaled
        if t == 0:
            s["D0"][0, p, win, :] = diag

    def rows0(h):
        return (8, 80, 16) if h > 4 else (12, 72, 24) if h > 0 else (16, 64, 16)

    level0.coefficients(s["K0"], s["S0"], c0, 1, 29, 4, 8, 80, 16, finish0)
    x, y = xa0, xb0
    for t in range(1, SWEEPS):
        h = 6 - t
        level0.sweep(x, y, b0, c0, weights[t], 7 - h, 23 + h, 8 + h, *rows0(h))
        x, y = y, x
    level0.residual(x, b0, c0, s["D0"], s["R0"], 7, 23, 8, *rows0(0))
    pre0 = x

    down1(s["R0"], 7, 16, s["B1"])
    round1 = side1(s["B1"], 2)
    start(round1)

    wait(coarse)
    level1 = Level(1, 0.25)
    level2 = Level(1, 0.0625)
    level3 = Level(1, 0.015625, closed=True)
    level4 = Level(1, 0.00390625)
    all3, all4 = (1, 9, 8, 8, 32, 32), (1, 5, 4, 8, 16, 16)

    def part1(h):
        return (8 - h, 16 + h, 8 + 2 * h) + ((8, 48, 48) if h > 4 else (12, 40, 40))

    def part2(h):
        return (1, 17, 16) + ((16, 32, 32) if h > 4 else (20, 24, 24))

    down4(s["K3"], s["K4"])
    down4(s["S3"], s["S4"])

    def finish(name):
        def keep(t, p, r, n, diag, inverse):
            s["D" + name][t, p, pl.ds(r, n), :] = diag
            s["I" + name][t, p, pl.ds(r, n), :] = inverse

        return keep

    level1.coefficients(s["K1"], s["S1"], s["C1"], 2, 22, 5, 8, 48, 48, finish("1"))
    wait(round1)
    merge1(s["B1"], 2)
    round1 = main1(s["B1"], 6)
    start(round1)

    pack0(lambda i: pre0[0, 7 + i, 16:80, :], s["PN0"].at[0])
    side_n0 = sides(s["PN0"], s["ZN0"])
    start(side_n0)
    level2.coefficients(s["K2"], s["S2"], s["C2"], 1, 17, 8, 16, 32, 32, finish("2"))
    level3.coefficients(s["K3"], s["S3"], s["C3"], *all3, finish("3"))
    level4.coefficients(s["K4"], s["S4"], s["C4"], *all4, finish("4"))

    def begin(name, low, high, size, row, rows, chunk):
        def block(first, count):
            for i in range(count):
                part = (0, first + i, pl.ds(row, rows), slice(None))
                scaled = s["B" + name][part] * s["I" + name][part]
                s["B" + name][part] = scaled
                s["XA" + name][part] = first_weight(name) * scaled

        groups(low, high, size, block)

    def first_weight(name):
        return cheb(BOTTOM_SWEEPS if name == "4" else SWEEPS)[0]

    wait(round1)
    begin("1", *part1(6))
    x, y = s["XA1"], s["XB1"]
    for t in range(1, SWEEPS):
        h = 6 - t
        level1.sweep(x, y, s["B1"], s["C1"], weights[t], *part1(h))
        x, y = y, x
    level1.residual(x, s["B1"], s["C1"], s["D1"], y, 8, 16, 8, 16, 32, 32)

    down2(y, s["B2"])
    round2 = side2(s["B2"], 2)
    start(round2)
    n32 = lane(32)
    for i in range(8):
        s["N1"][0, 8 + i, 16:48, :] = jnp.where(
            (n32 >= 32) & (n32 < 96), x[0, 8 + i, 16:48, :], 0.0
        )
    wait(round2)
    merge2(s["B2"], 2)
    round2 = main2(s["B2"])
    start(round2)
    side_n1 = side1(s["N1"], 3)
    start(side_n1)
    wait(round2)
    begin("2", *part2(6))
    x, y = s["XA2"], s["XB2"]
    for t in range(1, SWEEPS):
        level2.sweep(x, y, s["B2"], s["C2"], weights[t], *part2(6 - t))
        x, y = y, x
    level2.residual(x, s["B2"], s["C2"], s["D2"], s["R2"], 1, 17, 16, 24, 16, 16)

    down3(s["R2"], 2)
    round3 = side3(2)
    start(round3)
    n16 = lane(16)
    for i in range(4):
        p = 1 + 4 * gx + i
        s["N2"][0, p, 24:40, :] = jnp.where((n16 >= 48) & (n16 < 80), x[0, p, 24:40, :], 0.0)
    wait(round3)
    merge3(s["B3"], 2)
    round3 = main3(s["B3"])
    start(round3)

    side_n2 = side2(s["N2"], 3)
    start(side_n2)
    wait(side_n0)
    for g in range(2):
        s["GN0"][0, 1 + g, 8:72, :] = jnp.where(
            (n64 % 16) < 8, s["ZN0"][0, 0, g], s["ZN0"][1, 0, g]
        )
    ghosts = ghost0(s["GN0"])
    wait(side_n1)
    merge1(s["N1"], 3)
    wait(side_n2)
    merge2(s["N2"], 3)
    wait(round3)
    main_n2 = main2(s["N2"])
    start(main_n2)
    main_n1 = main1(s["N1"], 6)
    start(main_n1)
    start(ghosts)
    for i in range(16):
        s["N0"][0, 7 + i, 16:80, :] = pre0[0, 7 + i, 16:80, :]
    main_n0 = main0(s["N0"], 7, s["N0"], 6)
    start(main_n0)

    begin("3", *all3)
    x, y = s["XA3"], s["XB3"]
    for t in range(1, SWEEPS):
        level3.sweep(x, y, s["B3"], s["C3"], weights[t], *all3)
        x, y = y, x
    level3.residual(x, s["B3"], s["C3"], s["D3"], s["R3"], *all3)
    down4(s["R3"], s["B4"])

    begin("4", *all4)
    u, v = s["XA4"], s["XB4"]
    for weight in cheb(BOTTOM_SWEEPS)[1:]:
        level4.sweep(u, v, s["B4"], s["C4"], weight, *all4)
        u, v = v, u

    def spread(rows, planes, matrix, load, dst):
        value = product(jnp.concatenate([load(i) for i in range(planes)], axis=0), matrix)
        for i in range(planes):
            part = value[i * rows : (i + 1) * rows, :]
            dst[i, pl.ds(0, rows, stride=2), :] = part
            dst[i, pl.ds(1, rows, stride=2), :] = part

    fine = s["T"]
    spread(16, 4, doubling(0, 0, 0, 128), lambda i: u[0, 1 + i, 8:24, :], fine)
    for i in range(8):
        y[0, 1 + i, 8:40, :] = x[0, 1 + i, 8:40, :] + fine[i // 2, 0:32, :]
    for t in range(SWEEPS):
        x, y = y, x
        level3.sweep(x, y, s["B3"], s["C3"], weights[t], *all3)
    e3 = y

    wait(main_n2)
    rows3 = pl.ds(pl.multiple_of(8 * gy, 8), 24)
    spread(24, 8, doubling(16 * gz, 48, 16, 112), lambda i: e3[0, 1 + i, rows3, :], fine)
    y, x = s["XA2"], s["XB2"]
    for i in range(16):
        y[0, 1 + i, 12:52, :] = s["N2"][0, 1 + i, 12:52, :] + fine[i // 2, 4:44, :]
    for t in range(SWEEPS):
        x, y = y, x
        level2.sweep(x, y, s["B2"], s["C2"], weights[t], *part2(8 - t))
    e2 = y

    wait(main_n1)
    value = product(
        jnp.concatenate([e2[0, 1 + i, 20:44, :] for i in range(16)], axis=0),
        doubling(48, 32, 24, 104),
    )
    fine1 = s["T1"]
    pl.when(gx == 0)(lambda: clear(fine1, pl.ds(0, 4)))
    pl.when(gx == nx - 1)(lambda: clear(fine1, pl.ds(20, 4)))
    for i in range(16):
        part = value[i * 24 : (i + 1) * 24, :]
        fine1[4 + i, pl.ds(0, 24, stride=2), :] = part
        fine1[4 + i, pl.ds(1, 24, stride=2), :] = part
    y, x = s["XA1"], s["XB1"]
    for p in range(-6, 14):
        y[0, 8 + p, 8:56, :] = s["N1"][0, 8 + p, 8:56, :] + fine1[4 + 4 * gx + p // 2, 0:48, :]
    for t in range(SWEEPS):
        x, y = y, x
        h = 5 - t
        level1.sweep(x, y, s["B1"], s["C1"], weights[t], *part1(h))
    for i in range(8):
        s["E1"][0, 8 + i, 16:48, :] = jnp.where(
            (n32 >= 32) & (n32 < 96), y[0, 8 + i, 16:48, :], 0.0
        )
    round1 = side1(s["E1"], 4)
    start(round1)
    wait(ghosts)
    unpack0(s["GN0"].at[0], s["N0"])
    wait(round1)
    merge1(s["E1"], 4)
    round1 = main1(s["E1"], 3)
    start(round1)
    wait(main_n0)
    wait(round1)

    to_main = doubling(32, 0, 0, 128)
    to_side = doubling(32, -128, 0, 8) + doubling(32, 128, 120, 128)
    xa0 = s["S0"]
    for i in range(14):
        e = s["E1"][0, 5 + i, 12:52, :]
        for t, matrix in ((0, to_main), (1, to_side)):
            part = product(e, matrix)
            s["T0"][t, pl.ds(0, 40, stride=2), :] = part
            s["T0"][t, pl.ds(1, 40, stride=2), :] = part
            for o in range(2):
                p = 1 + 2 * i + o
                xa0[t, p, 8:88, :] = s["N0"][t, p, 8:88, :] + s["T0"][t, 0:80, :]
    x, y = s["XB0"], xa0
    for t in range(SWEEPS - 1):
        x, y = y, x
        h = 5 - t
        level0.sweep(x, y, b0, c0, weights[t], 7 - h, 23 + h, 8 + h, *rows0(h))

    def last(t, p, r, n, mid, value):
        out[p - 7, pl.ds(r - 16, n), :] = mid + weights[SWEEPS - 1] * value

    level0.defects(y, b0, c0, 7, 23, 8, *rows0(0), 1, last)


def scratch():
    shapes = {}
    for name in ("K0", "S0", "B0", "N0", "XB0"):
        shapes[name] = (2, 30, 96, 128)
    shapes["C0"] = (6, 2, 30, 96, 128)
    shapes["D0"], shapes["R0"] = (1, 30, 96, 128), (1, 23, 88, 128)
    shapes["P0"], shapes["Z0"], shapes["G0"] = (3, 2, 64, 128), (2, 3, 2, 64, 128), (3, 4, 80, 128)
    shapes["PN0"], shapes["ZN0"] = (1, 2, 64, 128), (2, 1, 2, 64, 128)
    shapes["GN0"] = (1, 4, 80, 128)
    shapes["T0"] = (2, 88, 128)
    for level, dims in (("1", (24, 64, 128)), ("2", (18, 64, 128)), ("3", (10, 48, 128)), ("4", (6, 32, 128))):
        for name in ("K", "S", "B", "I", "D", "XA", "XB"):
            shapes[name + level] = (1,) + dims
        shapes["C" + level] = (6, 1) + dims
    shapes["N1"] = shapes["E1"] = shapes["K1"]
    shapes["N2"] = shapes["R2"] = shapes["K2"]
    shapes["R3"] = shapes["K3"]
    shapes["P1"], shapes["Z1"] = (5, 32, 128), (5, 2, 32, 128)
    shapes["Z2"] = (4, 2, 4, 16, 128)
    shapes["Z3"] = (3, 8, 2, 8, 128)
    shapes["T"], shapes["T1"] = (8, 56, 128), (24, 56, 128)
    return {
        "send": pltpu.SemaphoreType.DMA((COPIES,)),
        "recv": pltpu.SemaphoreType.DMA((COPIES,)),
        "local": pltpu.SemaphoreType.DMA((3,)),
        **{name: pltpu.VMEM(shape, F32) for name, shape in shapes.items()},
    }


def on_device(rhs, kappa, sigma):
    return pl.pallas_call(
        kernel,
        out_shape=jax.ShapeDtypeStruct(rhs.shape, F32),
        in_specs=[pl.BlockSpec(memory_space=pl.ANY)] * 3,
        out_specs=pl.BlockSpec(memory_space=pltpu.VMEM),
        scratch_shapes=[scratch()],
        compiler_params=pltpu.CompilerParams(
            collective_id=0, has_side_effects=True, vmem_limit_bytes=63 * 2**20
        ),
    )(rhs, kappa, sigma)


def solution(mesh):
    placed = (P("gx", "gy", "gz"), P("gx", "gy", "gz"), P("gx", "gy", "gz"))
    return jax.shard_map(
        on_device, mesh=mesh, in_specs=placed, out_specs=P("gx", "gy", "gz"), check_vma=False
    )
```

```python
from functools import partial
import math

import jax
import jax.numpy as jnp
from jax import lax
from jax.experimental import pallas as pl
from jax.experimental.pallas import tpu as pltpu
from jax.sharding import PartitionSpec as P

LEVELS = 4
SWEEPS = 6
BOTTOM_SWEEPS = 8
MESH = pl.DeviceIdType.MESH
F32 = jnp.float32
COPIES = 148


def cheb(count):
    return [
        1.0 / (1.125 + 0.875 * math.cos(math.pi * (2 * t + 1) / (2 * count))) for t in range(count)
    ]


def lane(rows):
    return lax.broadcasted_iota(jnp.int32, (rows, 128), 1)


def turn(value, shift):
    shift = shift % 128
    return value if shift == 0 else pltpu.roll(value, shift, 1)


def product(value, matrix):
    return jnp.dot(value, matrix, precision=lax.Precision.HIGHEST, preferred_element_type=F32)


def halving(fine0, coarse0, count):
    i = lax.broadcasted_iota(jnp.int32, (128, 128), 0)
    j = lax.broadcasted_iota(jnp.int32, (128, 128), 1)
    offset = (i - fine0) - 2 * (j - coarse0)
    good = ((offset == 0) | (offset == 1)) & (j >= coarse0) & (j < coarse0 + count)
    return jnp.where(good, 0.125, 0.0).astype(F32)


def doubling(coarse0, fine0, low, high):
    i = lax.broadcasted_iota(jnp.int32, (128, 128), 0)
    j = lax.broadcasted_iota(jnp.int32, (128, 128), 1)
    offset = (j - fine0) - 2 * (i - coarse0)
    good = ((offset == 0) | (offset == 1)) & (j >= low) & (j < high)
    return jnp.where(good, 1.0, 0.0).astype(F32)


class Links:
    def __init__(self, send, recv):
        self.send, self.recv, self.used = send, recv, 0

    def copy(self, src, dst, target, send_ok=None, recv_ok=None, k=None):
        if k is None:
            k = self.used
            self.used += 1
        made = pltpu.make_async_remote_copy(
            src_ref=src,
            dst_ref=dst,
            send_sem=self.send.at[k],
            recv_sem=self.recv.at[k],
            device_id=target,
            device_id_type=MESH,
        )
        return made, send_ok, recv_ok


def given(flag, action):
    if flag is None:
        action()
    else:
        pl.when(flag)(action)


def start(copies):
    for made, send_ok, _ in copies:
        given(send_ok, made.start)


def wait(copies):
    for made, _, recv_ok in copies:
        given(recv_ok, made.wait_recv)
    for made, send_ok, _ in copies:
        given(send_ok, made.wait_send)


def both(a, b):
    if a is None:
        return b
    return a if b is None else a & b


def groups(low, high, size, action):
    whole = (high - low) // size
    if whole == 1:
        action(low, size)
    elif whole:

        def body(i, carry):
            action(low + size * i, size)
            return carry

        lax.fori_loop(0, whole, body, 0)
    rest = (high - low) % size
    if rest:
        action(high - rest, rest)


class Level:
    def __init__(self, tiles, scale, closed=False):
        self.tiles, self.scale, self.closed = tiles, scale, closed

    def beside(self, values):
        n = lane(values[0].shape[0])
        left = [turn(v, 1) for v in values]
        right = [turn(v, -1) for v in values]
        if self.tiles == 2:
            left = [jnp.where(n == 0, left[1 - t], left[t]) for t in range(2)]
            right = [jnp.where(n == 127, right[1 - t], right[t]) for t in range(2)]
        return left, right

    def around(self, ref, p, count, row, rows, tiles):
        win = pl.ds(row, rows)
        mid = [[ref[t, p + i - 1, win, :] for i in range(count + 2)] for t in range(tiles)]
        mid += [[None] + [ref[t, p + i, win, :] for i in range(count)] for t in range(tiles, self.tiles)]
        found = []
        for i in range(count):
            left, right = self.beside([mid[t][i + 1] for t in range(self.tiles)])
            for t in range(tiles):
                near = [
                    mid[t][i + 2],
                    mid[t][i],
                    ref[t, p + i, pl.ds(row + 1, rows), :],
                    ref[t, p + i, pl.ds(row - 1, rows), :],
                    left[t],
                    right[t],
                ]
                found.append((t, p + i, mid[t][i + 1], near))
        return found

    def coefficients(self, kappa, sigma, coef, low, high, size, row, rows, chunk, finish):
        def block(first, count):
            for start_row in range(row, row + rows, chunk):
                win = pl.ds(start_row, chunk)
                n = lane(chunk)
                for t, p, k, near in self.around(kappa, first, count, start_row, chunk, self.tiles):
                    if self.closed:
                        near[4] = jnp.where(n == 0, 0.0, near[4])
                        near[5] = jnp.where(n == 127, 0.0, near[5])
                    face = [(0.5 * self.scale) * (k + j) for j in near]
                    diag = (face[0] + face[1]) + (face[2] + face[3]) + (face[4] + face[5])
                    diag = diag + sigma[t, p, win, :]
                    inverse = jnp.where(k > 0.0, 1.0 / diag, 0.0)
                    if self.closed:
                        face[4] = jnp.where(n == 0, 0.0, face[4])
                        face[5] = jnp.where(n == 127, 0.0, face[5])
                    for j in range(6):
                        coef[j, t, p, win, :] = face[j] * inverse
                    finish(t, p, start_row, chunk, diag, inverse)

        groups(low, high, size, block)

    def defects(self, x, rhs, coef, low, high, size, row, rows, chunk, tiles, use):
        def block(first, count):
            for start_row in range(row, row + rows, chunk):
                win = pl.ds(start_row, chunk)
                found = []
                for t, p, mid, near in self.around(x, first, count, start_row, chunk, tiles):
                    c = [coef[j, t, p, win, :] for j in range(6)]
                    a = (c[0] * near[0] + c[1] * near[1]) + (c[2] * near[2] + c[3] * near[3])
                    b = (rhs[t, p, win, :] - mid) + (c[4] * near[4] + c[5] * near[5])
                    found.append((t, p, mid, a + b))
                for t, p, mid, value in found:
                    use(t, p, start_row, chunk, mid, value)

        groups(low, high, size, block)

    def sweep(self, src, dst, rhs, coef, weight, low, high, size, row, rows, chunk):
        def use(t, p, r, n, mid, value):
            dst[t, p, pl.ds(r, n), :] = mid + weight * value

        self.defects(src, rhs, coef, low, high, size, row, rows, chunk, self.tiles, use)

    def residual(self, x, rhs, coef, diag, dst, low, high, size, row, rows, chunk):
        def use(t, p, r, n, mid, value):
            dst[0, p, pl.ds(r, n), :] = diag[0, p, pl.ds(r, n), :] * value

        self.defects(x, rhs, coef, low, high, size, row, rows, chunk, 1, use)


def restrict(load, planes, matrix, store):
    sums = [
        load(2 * i, 0) + load(2 * i, 1) + load(2 * i + 1, 0) + load(2 * i + 1, 1)
        for i in range(planes)
    ]
    rows = sums[0].shape[0]
    out = product(jnp.concatenate(sums, axis=0), matrix)
    for i in range(planes):
        store(i, out[i * rows : (i + 1) * rows, :])


def kernel(rhs, kappa, sigma, out, s):
    gx, gy, gz = lax.axis_index("gx"), lax.axis_index("gy"), lax.axis_index("gz")
    nx, ny, nz = 4, 4, 8
    links = Links(s["send"], s["recv"])
    s = dict(s)
    for level in "123":
        s["K" + level] = s["KS" + level].at[pl.ds(0, 1)]
        s["S" + level] = s["KS" + level].at[pl.ds(1, 1)]
    has = {
        ("x", 1): gx < nx - 1,
        ("x", -1): gx > 0,
        ("y", 1): gy < ny - 1,
        ("y", -1): gy > 0,
        ("z", 1): gz < nz - 1,
        ("z", -1): gz > 0,
        ("x", 0): None,
        ("y", 0): None,
    }

    def clear(ref, *index):
        part = ref.at[index] if index else ref
        part[...] = jnp.zeros(part.shape, F32)

    def clear_edges(ref, planes, rows):
        total = ref.shape[1]
        pl.when(gx == 0)(lambda: clear(ref, 0, pl.ds(0, planes[0])))
        pl.when(gx == nx - 1)(lambda: clear(ref, 0, pl.ds(planes[1], total - planes[1])))
        pl.when(gy == 0)(lambda: clear(ref, 0, slice(None), pl.ds(rows[0], rows[1])))
        pl.when(gy == ny - 1)(lambda: clear(ref, 0, slice(None), pl.ds(rows[2], rows[1])))

    for name in ("K0", "S0", "B0", "N0"):
        clear_edges(s[name], (7, 23), (8, 8, 80))
    for name in ("K1", "S1", "B1", "N1", "E1"):
        clear_edges(s[name], (8, 16), (8, 8, 48))
    every = slice(None)
    pl.when(gy == 0)(lambda: clear(s["Q2"], every, every, every, pl.ds(0, 16)))
    pl.when(gy == ny - 1)(lambda: clear(s["Q2"], every, every, every, pl.ds(32, 16)))
    for name in ("K2", "XA2", "XB2"):
        clear(s[name], 0, 0)
        clear(s[name], 0, 17)
    for name, planes, rows in (("3", 8, 32), ("4", 4, 16)):
        for field in ("K", "XA", "XB"):
            ref = s[field + name]
            clear(ref, 0, 0)
            clear(ref, 0, planes + 1)
            clear(ref, 0, slice(None), pl.ds(0, 8))
            clear(ref, 0, slice(None), pl.ds(8 + rows, 8))
    for name in ("G0", "GN0"):
        clear(s[name])

    @pl.when((gz == 0) | (gz == nz - 1))
    def _():
        for name in ("Z0", "ZN0", "Z1", "Z2"):
            clear(s[name])

    barrier = pltpu.get_barrier_semaphore()
    plane_mates = [
        (lax.rem(gx + i, nx), lax.rem(gy + j, ny), gz)
        for i in range(nx)
        for j in range(ny)
        if i or j
    ]
    line_mates = [(gx, gy, lax.rem(gz + i, nz)) for i in range(1, nz)]
    for mate in plane_mates + line_mates:
        pl.semaphore_signal(barrier, inc=1, device_id=mate, device_id_type=MESH)

    around = [(dx, dy) for dx in (1, -1, 0) for dy in (0, 1, -1) if dx or dy]

    def neighbours(make, first=None):
        copies = []
        for m, (dx, dy) in enumerate(around):
            src, dst = make(dx, dy)
            copies.append(
                links.copy(
                    src,
                    dst,
                    (gx + dx, gy + dy, gz),
                    both(has["x", dx], has["y", dy]),
                    both(has["x", -dx], has["y", -dy]),
                    None if first is None else first + m,
                )
            )
        return copies

    def sides(src, slots):
        return [
            links.copy(src, slots.at[0], (gx, gy, gz + 1), has["z", 1], has["z", -1]),
            links.copy(src, slots.at[1], (gx, gy, gz - 1), has["z", -1], has["z", 1]),
        ]

    def main0(src, first, ref, h, k=None):
        def make(dx, dy):
            sp = {1: (first + 16 - h, h), -1: (first, h), 0: (first, 16)}[dx]
            dp = {1: (7 - h, h), -1: (23, h), 0: (7, 16)}[dx]
            sr = {1: (56, 8), -1: (0, 8), 0: (0, 64)}[dy]
            dr = {1: (8, 8), -1: (80, 8), 0: (16, 64)}[dy]
            base = 0 if src is not ref else 16
            source = src.at[pl.ds(*sp), pl.ds(base + sr[0], sr[1])] if base == 0 else src.at[
                0, pl.ds(*sp), pl.ds(base + sr[0], sr[1])
            ]
            return source, ref.at[0, pl.ds(*dp), pl.ds(*dr)]

        return neighbours(make, k)

    inner = [
        pltpu.make_async_copy(src, s[name].at[0, pl.ds(7, 16), pl.ds(16, 64)], s["local"].at[k])
        for k, (src, name) in enumerate(((kappa, "K0"), (sigma, "S0"), (rhs, "B0")))
    ]
    for made in inner:
        made.start()
    mains = main0(kappa, 0, s["K0"], 7) + main0(sigma, 0, s["S0"], 6)
    main_b = main0(rhs, 0, s["B0"], 6)
    for made in inner:
        made.wait()

    def pack0(load, dst):
        n = lane(64)
        for g in range(2):
            total = jnp.zeros((64, 128), F32)
            for q in range(8):
                moved = turn(load(8 * g + q), 16 * q + 8)
                total = jnp.where((n >= 16 * q) & (n < 16 * q + 16), moved, total)
            dst[g, :, :] = total

    for a, name in enumerate(("K0", "S0", "B0")):
        pack0(lambda i, ref=s[name]: ref[0, 7 + i, 16:80, :], s["P0"].at[a])
    side0 = sides(s["P0"], s["Z0"])
    pl.semaphore_wait(barrier, len(plane_mates + line_mates))
    start(mains)
    start(main_b)
    start(side0)

    to1 = halving(0, 32, 64)
    to2 = halving(32, 48, 32)
    to3 = halving(48, 16 * gz, 16)
    to4 = halving(0, 0, 64)
    own2 = pl.ds(1 + 4 * gx, 4)
    own3 = pl.ds(1 + 2 * gx, 2)
    row3 = pl.ds(pl.multiple_of(8 + 8 * gy, 8), 8)

    def down1(src, first, row, dst):
        def store(i, v):
            dst[0, 8 + i, 16:48, :] = v

        restrict(lambda i, o: src[0, first + i, pl.ds(row + o, 32, stride=2), :], 8, to1, store)

    def down2(src, dst):
        def store(i, v):
            dst[0, 1 + 4 * gx + i, 24:40, :] = v

        restrict(lambda i, o: src[0, 8 + i, pl.ds(16 + o, 16, stride=2), :], 4, to2, store)

    def down3(src, use):
        def store(i, v):
            s["Z3"][gz, use, i, :, :] = v

        restrict(
            lambda i, o: src[0, 1 + 4 * gx + i, pl.ds(24 + o, 8, stride=2), :], 2, to3, store
        )

    def down4(src, dst):
        def store(i, v):
            dst[0, 1 + i, 8:24, :] = v

        restrict(lambda i, o: src[0, 1 + i, pl.ds(8 + o, 16, stride=2), :], 4, to4, store)

    def pack1(ref, use):
        n = lane(32)
        total = jnp.zeros((32, 128), F32)
        for q in range(8):
            v = ref[0, 8 + q, 16:48, :]
            v = turn(v + turn(v, 64), 16 * q - 24)
            total = jnp.where((n >= 16 * q) & (n < 16 * q + 16), v, total)
        s["P1"][use, :, :] = total

    def side1(use, count=1):
        part = pl.ds(use, count)
        return sides(s["P1"].at[part], s["Z1"].at[:, part])

    def merge1(ref, use):
        n = lane(32)
        ghosts = jnp.where((n % 16) < 8, s["Z1"][0, use], s["Z1"][1, use])
        for q in range(8):
            low = turn(ghosts, 24 - 16 * q)
            high = turn(ghosts, 24 - 16 * q + 64)
            v = ref[0, 8 + q, 16:48, :]
            v = jnp.where((n >= 24) & (n < 32), low, v)
            ref[0, 8 + q, 16:48, :] = jnp.where((n >= 96) & (n < 104), high, v)

    def main1(ref, h, k=None):
        def make(dx, dy):
            sp = {1: (16 - h, h), -1: (8, h), 0: (8, 8)}[dx]
            dp = {1: (8 - h, h), -1: (16, h), 0: (8, 8)}[dx]
            sr = {1: (40, 8), -1: (16, 8), 0: (16, 32)}[dy]
            dr = {1: (8, 8), -1: (48, 8), 0: (16, 32)}[dy]
            return ref.at[:, pl.ds(*sp), pl.ds(*sr)], ref.at[:, pl.ds(*dp), pl.ds(*dr)]

        return neighbours(make, k)

    def side2(ref, use, count=1):
        return sides(ref.at[:, own2, pl.ds(24, 16)], s["Z2"].at[:, pl.ds(use, count)])

    def merge2(ref, use):
        n = lane(16)
        whole = [
            ref[0, 1 + 4 * gx + i, 24:40, :]
            + turn(s["Z2"][0, use, i], -32)
            + turn(s["Z2"][1, use, i], 32)
            for i in range(4)
        ]
        for i in range(2):
            s["Q2"][use, gx, i, 16:32, :] = jnp.where(
                n < 64, turn(whole[i], -32), turn(whole[i + 2], 32)
            )

    def main2(use, count=1, first=None):
        copies = []
        for i in range(nx):
            for dy in (0, 1, -1):
                if i == 0 and dy == 0:
                    continue
                dr = {1: (0, 16), -1: (32, 16), 0: (16, 16)}[dy]
                part = s["Q2"].at[pl.ds(use, count), gx]
                copies.append(
                    links.copy(
                        part.at[:, :, pl.ds(16, 16)],
                        part.at[:, :, pl.ds(*dr)],
                        (lax.rem(gx + i, nx), gy + dy, gz),
                        has["y", dy],
                        has["y", -dy],
                        None if first is None else first + len(copies),
                    )
                )
        return copies

    def spread2(use, ref):
        n = lane(48)
        inside = (n >= 32) & (n < 96)
        for g in range(nx):
            for i in range(2):
                v = s["Q2"][use, g, i]
                ref[0, 1 + 4 * g + i, 8:56, :] = jnp.where(inside, turn(v, 32), 0.0)
                ref[0, 3 + 4 * g + i, 8:56, :] = jnp.where(inside, turn(v, -32), 0.0)

    def side3(use, count=1):
        part = s["Z3"].at[gz, pl.ds(use, count)]
        return [links.copy(part, part, mate) for mate in line_mates]

    def merge3(ref, use):
        for i in range(2):
            total = s["Z3"][0, use, i]
            for q in range(1, nz):
                total = total + s["Z3"][q, use, i]
            ref[0, 1 + 2 * gx + i, row3, :] = total

    def main3(ref):
        part = ref.at[:, own3, row3]
        return [links.copy(part, part, mate) for mate in plane_mates]

    down1(s["K0"], 7, 16, s["K1"])
    down1(s["S0"], 7, 16, s["S1"])
    pack1(s["K1"], 0)
    pack1(s["S1"], 1)
    side_ks1 = side1(0, 2)
    start(side_ks1)
    down2(s["K1"], s["K2"])
    down2(s["S1"], s["S2"])
    side_ks2 = side2(s["KS2"], 0, 2)
    start(side_ks2)
    down3(s["K2"], 0)
    down3(s["S2"], 1)
    side_ks3 = side3(0, 2)
    start(side_ks3)

    wait(side0)
    n64 = lane(64)
    for a in range(3):
        for g in range(2):
            s["G0"][a, 1 + g, 8:72, :] = jnp.where(
                (n64 % 16) < 8, s["Z0"][0, a, g], s["Z0"][1, a, g]
            )

    def ghost0(ref, k=None):
        def make(dx, dy):
            sg = {1: (2, 1), -1: (1, 1), 0: (1, 2)}[dx]
            dg = {1: (0, 1), -1: (3, 1), 0: (1, 2)}[dx]
            sr = {1: (64, 8), -1: (8, 8), 0: (8, 64)}[dy]
            dr = {1: (0, 8), -1: (72, 8), 0: (8, 64)}[dy]
            return ref.at[:, pl.ds(*sg), pl.ds(*sr)], ref.at[:, pl.ds(*dg), pl.ds(*dr)]

        return neighbours(make, k)

    def unpack0(src, ref):
        n = lane(80)
        edge = (n < 8) | (n >= 120)

        for g in range(4):
            v = src[g]
            for q in range(8):
                p = 8 * g + q - 1
                if 0 <= p < 30:
                    ref[1, p, 8:88, :] = jnp.where(edge, turn(v, -16 * q - 8), 0.0)

    ghosts = ghost0(s["G0"])
    start(ghosts)

    wait(side_ks1)
    merge1(s["K1"], 0)
    merge1(s["S1"], 1)
    main_ks1 = main1(s["KS1"], 7)
    start(main_ks1)
    wait(side_ks2)
    merge2(s["K2"], 0)
    merge2(s["S2"], 1)
    first_main2 = links.used
    main_ks2 = main2(0, 2)
    start(main_ks2)
    wait(side_ks3)
    merge3(s["K3"], 0)
    merge3(s["S3"], 1)
    main_ks3 = main3(s["KS3"])
    start(main_ks3)

    wait(ghosts)
    for a, name in enumerate(("K0", "S0", "B0")):
        unpack0(s["G0"].at[a], s[name])
    wait(mains)

    weights = cheb(SWEEPS)
    level0 = Level(2, 1.0)
    c0, b0, xa0, xb0 = s["C0"], s["B0"], s["S0"], s["XB0"]

    def finish0(t, p, r, n, diag, inverse):
        win = pl.ds(r, n)
        xa0[t, p, win, :] = inverse
        if t == 0:
            s["D0"][0, p, win, :] = diag

    def rows0(h):
        return (8, 80, 16) if h > 4 else (12, 72, 24) if h > 0 else (16, 64, 16)

    level0.coefficients(s["K0"], s["S0"], c0, 1, 29, 4, 8, 80, 16, finish0)
    wait(main_b)

    def begin0(first, count):
        for t in range(2):
            for i in range(count):
                part = (t, first + i, pl.ds(8, 80), slice(None))
                scaled = b0[part] * xa0[part]
                b0[part] = scaled
                xa0[part] = weights[0] * scaled

    groups(1, 29, 4, begin0)
    x, y = xa0, xb0
    for t in range(1, SWEEPS):
        h = 6 - t
        level0.sweep(x, y, b0, c0, weights[t], 7 - h, 23 + h, 8 + h, *rows0(h))
        x, y = y, x
    level0.residual(x, b0, c0, s["D0"], s["R0"], 7, 23, 8, *rows0(0))
    pre0 = x

    down1(s["R0"], 7, 16, s["B1"])
    pack1(s["B1"], 2)
    round1 = side1(2)
    start(round1)
    pack0(lambda i: pre0[0, 7 + i, 16:80, :], s["PN0"].at[0])
    side_n0 = sides(s["PN0"], s["ZN0"])
    start(side_n0)

    level1 = Level(1, 0.25)
    level2 = Level(1, 0.0625)
    level3 = Level(1, 0.015625, closed=True)
    level4 = Level(1, 0.00390625)
    all3, all4 = (1, 9, 8, 8, 32, 32), (1, 5, 4, 8, 16, 16)

    def part1(h):
        return (8 - h, 16 + h, 8 + 2 * h) + ((8, 48, 48) if h > 4 else (12, 40, 40))

    def part2(h):
        return (1, 17, 16) + ((16, 32, 32) if h > 4 else (20, 24, 24))

    def finish(name):
        def keep(t, p, r, n, diag, inverse):
            s["D" + name][t, p, pl.ds(r, n), :] = diag
            s["I" + name][t, p, pl.ds(r, n), :] = inverse

        return keep

    wait(main_ks1)
    level1.coefficients(s["K1"], s["S1"], s["C1"], 2, 22, 5, 8, 48, 48, finish("1"))
    wait(round1)
    merge1(s["B1"], 2)
    round1 = main1(s["B1"], 6)
    start(round1)

    for i in range(16):
        s["N0"][0, 7 + i, 16:80, :] = pre0[0, 7 + i, 16:80, :]
    main_n0 = main0(s["N0"], 7, s["N0"], 6)
    start(main_n0)
    wait(side_n0)
    for g in range(2):
        s["GN0"][0, 1 + g, 8:72, :] = jnp.where(
            (n64 % 16) < 8, s["ZN0"][0, 0, g], s["ZN0"][1, 0, g]
        )
    ghosts = ghost0(s["GN0"])
    start(ghosts)
    wait(main_ks2)
    spread2(0, s["K2"])
    spread2(1, s["S2"])
    wait(main_ks3)
    down4(s["K3"], s["K4"])
    down4(s["S3"], s["S4"])
    level2.coefficients(s["K2"], s["S2"], s["C2"], 1, 17, 8, 16, 32, 32, finish("2"))
    level3.coefficients(s["K3"], s["S3"], s["C3"], *all3, finish("3"))
    level4.coefficients(s["K4"], s["S4"], s["C4"], *all4, finish("4"))

    def begin(name, low, high, size, row, rows, chunk):
        def block(first, count):
            for i in range(count):
                part = (0, first + i, pl.ds(row, rows), slice(None))
                scaled = s["B" + name][part] * s["I" + name][part]
                s["B" + name][part] = scaled
                s["XA" + name][part] = first_weight(name) * scaled

        groups(low, high, size, block)

    def first_weight(name):
        return cheb(BOTTOM_SWEEPS if name == "4" else SWEEPS)[0]

    wait(round1)
    begin("1", *part1(6))
    x, y = s["XA1"], s["XB1"]
    for t in range(1, SWEEPS):
        h = 6 - t
        level1.sweep(x, y, s["B1"], s["C1"], weights[t], *part1(h))
        x, y = y, x
    level1.residual(x, s["B1"], s["C1"], s["D1"], y, 8, 16, 8, 16, 32, 32)

    down2(y, s["B2"])
    round2 = side2(s["B2"], 2)
    start(round2)
    n32 = lane(32)
    for i in range(8):
        s["N1"][0, 8 + i, 16:48, :] = jnp.where(
            (n32 >= 32) & (n32 < 96), x[0, 8 + i, 16:48, :], 0.0
        )
    pack1(s["N1"], 3)
    side_n1 = side1(3)
    start(side_n1)
    wait(round2)
    merge2(s["B2"], 2)
    round2 = main2(2)
    start(round2)
    wait(side_n1)
    merge1(s["N1"], 3)
    main_n1 = main1(s["N1"], 6, 0)
    start(main_n1)
    wait(round2)
    spread2(2, s["B2"])
    begin("2", *part2(6))
    x, y = s["XA2"], s["XB2"]
    for t in range(1, SWEEPS):
        level2.sweep(x, y, s["B2"], s["C2"], weights[t], *part2(6 - t))
        x, y = y, x
    level2.residual(x, s["B2"], s["C2"], s["D2"], s["R2"], 1, 17, 16, 24, 16, 16)

    down3(s["R2"], 2)
    round3 = side3(2)
    start(round3)
    n16 = lane(16)
    for i in range(4):
        p = 1 + 4 * gx + i
        s["N2"][0, p, 24:40, :] = jnp.where((n16 >= 48) & (n16 < 80), x[0, p, 24:40, :], 0.0)
    side_n2 = side2(s["N2"], 3)
    start(side_n2)
    wait(round3)
    merge3(s["B3"], 2)
    round3 = main3(s["B3"])
    start(round3)
    wait(side_n2)
    merge2(s["N2"], 3)
    wait(round3)
    main_n2 = main2(3, 1, first_main2)
    start(main_n2)

    begin("3", *all3)
    x, y = s["XA3"], s["XB3"]
    for t in range(1, SWEEPS):
        level3.sweep(x, y, s["B3"], s["C3"], weights[t], *all3)
        x, y = y, x
    level3.residual(x, s["B3"], s["C3"], s["D3"], s["R3"], *all3)
    down4(s["R3"], s["B4"])

    begin("4", *all4)
    u, v = s["XA4"], s["XB4"]
    for weight in cheb(BOTTOM_SWEEPS)[1:]:
        level4.sweep(u, v, s["B4"], s["C4"], weight, *all4)
        u, v = v, u

    def spread(rows, planes, matrix, load, dst):
        value = product(jnp.concatenate([load(i) for i in range(planes)], axis=0), matrix)
        for i in range(planes):
            part = value[i * rows : (i + 1) * rows, :]
            dst[i, pl.ds(0, rows, stride=2), :] = part
            dst[i, pl.ds(1, rows, stride=2), :] = part

    fine = s["T"]
    spread(16, 4, doubling(0, 0, 0, 128), lambda i: u[0, 1 + i, 8:24, :], fine)
    for i in range(8):
        y[0, 1 + i, 8:40, :] = x[0, 1 + i, 8:40, :] + fine[i // 2, 0:32, :]
    for t in range(SWEEPS):
        x, y = y, x
        level3.sweep(x, y, s["B3"], s["C3"], weights[t], *all3)
    e3 = y

    wait(main_n2)
    spread2(3, s["N2"])
    rows3 = pl.ds(pl.multiple_of(8 * gy, 8), 24)
    spread(24, 8, doubling(16 * gz, 48, 16, 112), lambda i: e3[0, 1 + i, rows3, :], fine)
    y, x = s["XA2"], s["XB2"]
    for i in range(16):
        y[0, 1 + i, 12:52, :] = s["N2"][0, 1 + i, 12:52, :] + fine[i // 2, 4:44, :]
    for t in range(SWEEPS):
        x, y = y, x
        level2.sweep(x, y, s["B2"], s["C2"], weights[t], *part2(8 - t))
    e2 = y

    wait(main_n1)
    value = product(
        jnp.concatenate([e2[0, 1 + i, 20:44, :] for i in range(16)], axis=0),
        doubling(48, 32, 24, 104),
    )
    fine1 = s["T1"]
    pl.when(gx == 0)(lambda: clear(fine1, pl.ds(0, 4)))
    pl.when(gx == nx - 1)(lambda: clear(fine1, pl.ds(20, 4)))
    for i in range(16):
        part = value[i * 24 : (i + 1) * 24, :]
        fine1[4 + i, pl.ds(0, 24, stride=2), :] = part
        fine1[4 + i, pl.ds(1, 24, stride=2), :] = part
    y, x = s["XA1"], s["XB1"]
    for p in range(-6, 14):
        y[0, 8 + p, 8:56, :] = s["N1"][0, 8 + p, 8:56, :] + fine1[4 + 4 * gx + p // 2, 0:48, :]
    for t in range(SWEEPS):
        x, y = y, x
        h = 5 - t
        level1.sweep(x, y, s["B1"], s["C1"], weights[t], *part1(h))
    for i in range(8):
        s["E1"][0, 8 + i, 16:48, :] = jnp.where(
            (n32 >= 32) & (n32 < 96), y[0, 8 + i, 16:48, :], 0.0
        )
    pack1(s["E1"], 4)
    round1 = side1(4)
    start(round1)
    wait(ghosts)
    unpack0(s["GN0"].at[0], s["N0"])
    wait(round1)
    merge1(s["E1"], 4)
    round1 = main1(s["E1"], 3, 8)
    start(round1)
    wait(main_n0)
    wait(round1)

    to_main = doubling(32, 0, 0, 128)
    to_side = doubling(32, -128, 0, 8) + doubling(32, 128, 120, 128)
    xa0 = s["S0"]
    for i in range(14):
        e = s["E1"][0, 5 + i, 12:52, :]
        for t, matrix in ((0, to_main), (1, to_side)):
            part = product(e, matrix)
            s["T0"][t, pl.ds(0, 40, stride=2), :] = part
            s["T0"][t, pl.ds(1, 40, stride=2), :] = part
            for o in range(2):
                p = 1 + 2 * i + o
                xa0[t, p, 8:88, :] = s["N0"][t, p, 8:88, :] + s["T0"][t, 0:80, :]
    x, y = s["XB0"], xa0
    for t in range(SWEEPS - 1):
        x, y = y, x
        h = 5 - t
        level0.sweep(x, y, b0, c0, weights[t], 7 - h, 23 + h, 8 + h, *rows0(h))

    def last(t, p, r, n, mid, value):
        out[p - 7, pl.ds(r - 16, n), :] = mid + weights[SWEEPS - 1] * value

    level0.defects(y, b0, c0, 7, 23, 8, *rows0(0), 1, last)


def scratch():
    shapes = {}
    for name in ("K0", "S0", "B0", "N0", "XB0"):
        shapes[name] = (2, 30, 96, 128)
    shapes["C0"] = (6, 2, 30, 96, 128)
    shapes["D0"], shapes["R0"] = (1, 30, 96, 128), (1, 23, 88, 128)
    shapes["P0"], shapes["Z0"], shapes["G0"] = (3, 2, 64, 128), (2, 3, 2, 64, 128), (3, 4, 80, 128)
    shapes["PN0"], shapes["ZN0"] = (1, 2, 64, 128), (2, 1, 2, 64, 128)
    shapes["GN0"] = (1, 4, 80, 128)
    shapes["T0"] = (2, 88, 128)
    for level, dims in (("1", (24, 64, 128)), ("2", (18, 64, 128)), ("3", (10, 48, 128)), ("4", (6, 32, 128))):
        for name in ("K", "S", "B", "I", "D", "XA", "XB"):
            shapes[name + level] = (1,) + dims
        if level != "4":
            del shapes["K" + level], shapes["S" + level]
            shapes["KS" + level] = (2,) + dims
        shapes["C" + level] = (6, 1) + dims
    shapes["N1"] = shapes["E1"] = shapes["B1"]
    shapes["N2"] = shapes["R2"] = shapes["B2"]
    shapes["R3"] = shapes["B3"]
    shapes["P1"], shapes["Z1"] = (5, 32, 128), (2, 5, 32, 128)
    shapes["Z2"], shapes["Q2"] = (2, 4, 4, 16, 128), (4, 4, 2, 48, 128)
    shapes["Z3"] = (8, 3, 2, 8, 128)
    shapes["T"], shapes["T1"] = (8, 56, 128), (24, 56, 128)
    return {
        "send": pltpu.SemaphoreType.DMA((COPIES,)),
        "recv": pltpu.SemaphoreType.DMA((COPIES,)),
        "local": pltpu.SemaphoreType.DMA((3,)),
        **{name: pltpu.VMEM(shape, F32) for name, shape in shapes.items()},
    }


def on_device(rhs, kappa, sigma):
    return pl.pallas_call(
        kernel,
        out_shape=jax.ShapeDtypeStruct(rhs.shape, F32),
        in_specs=[pl.BlockSpec(memory_space=pl.ANY)] * 3,
        out_specs=pl.BlockSpec(memory_space=pltpu.VMEM),
        scratch_shapes=[scratch()],
        compiler_params=pltpu.CompilerParams(
            collective_id=0, has_side_effects=True, vmem_limit_bytes=63 * 2**20
        ),
    )(rhs, kappa, sigma)


def solution(mesh):
    placed = (P("gx", "gy", "gz"), P("gx", "gy", "gz"), P("gx", "gy", "gz"))
    return jax.shard_map(
        on_device, mesh=mesh, in_specs=placed, out_specs=P("gx", "gy", "gz"), check_vma=False
    )
```

```python
from functools import partial
import math

import jax
import jax.numpy as jnp
from jax import lax
from jax.experimental import pallas as pl
from jax.experimental.pallas import tpu as pltpu
from jax.sharding import PartitionSpec as P

LEVELS = 4
SWEEPS = 6
BOTTOM_SWEEPS = 8
MESH = pl.DeviceIdType.MESH
F32 = jnp.float32
COPIES = 132


def cheb(count):
    return [
        1.0 / (1.125 + 0.875 * math.cos(math.pi * (2 * t + 1) / (2 * count))) for t in range(count)
    ]


def lane(rows):
    return lax.broadcasted_iota(jnp.int32, (rows, 128), 1)


def turn(value, shift):
    shift = shift % 128
    return value if shift == 0 else pltpu.roll(value, shift, 1)


def product(value, matrix):
    return jnp.dot(value, matrix, precision=lax.Precision.HIGHEST, preferred_element_type=F32)


def halving(fine0, coarse0, count):
    i = lax.broadcasted_iota(jnp.int32, (128, 128), 0)
    j = lax.broadcasted_iota(jnp.int32, (128, 128), 1)
    offset = (i - fine0) - 2 * (j - coarse0)
    good = ((offset == 0) | (offset == 1)) & (j >= coarse0) & (j < coarse0 + count)
    return jnp.where(good, 0.125, 0.0).astype(F32)


def doubling(coarse0, fine0, low, high):
    i = lax.broadcasted_iota(jnp.int32, (128, 128), 0)
    j = lax.broadcasted_iota(jnp.int32, (128, 128), 1)
    offset = (j - fine0) - 2 * (i - coarse0)
    good = ((offset == 0) | (offset == 1)) & (j >= low) & (j < high)
    return jnp.where(good, 1.0, 0.0).astype(F32)


class Links:
    def __init__(self, send, recv):
        self.send, self.recv, self.used = send, recv, 0

    def copy(self, src, dst, target, send_ok=None, recv_ok=None, k=None):
        if k is None:
            k = self.used
            self.used += 1
        made = pltpu.make_async_remote_copy(
            src_ref=src,
            dst_ref=dst,
            send_sem=self.send.at[k],
            recv_sem=self.recv.at[k],
            device_id=target,
            device_id_type=MESH,
        )
        return made, send_ok, recv_ok


def given(flag, action):
    if flag is None:
        action()
    else:
        pl.when(flag)(action)


def start(copies):
    for made, send_ok, _ in copies:
        given(send_ok, made.start)


def wait(copies):
    for made, _, recv_ok in copies:
        given(recv_ok, made.wait_recv)
    for made, send_ok, _ in copies:
        given(send_ok, made.wait_send)


def both(a, b):
    if a is None:
        return b
    return a if b is None else a & b


def groups(low, high, size, action):
    whole = (high - low) // size
    if whole == 1:
        action(low, size)
    elif whole:

        def body(i, carry):
            action(low + size * i, size)
            return carry

        lax.fori_loop(0, whole, body, 0)
    rest = (high - low) % size
    if rest:
        action(high - rest, rest)


class Level:
    def __init__(self, tiles, scale, closed=False):
        self.tiles, self.scale, self.closed = tiles, scale, closed

    def beside(self, values):
        n = lane(values[0].shape[0])
        left = [turn(v, 1) for v in values]
        right = [turn(v, -1) for v in values]
        if self.tiles == 2:
            left = [jnp.where(n == 0, left[1 - t], left[t]) for t in range(2)]
            right = [jnp.where(n == 127, right[1 - t], right[t]) for t in range(2)]
        return left, right

    def around(self, ref, p, count, row, rows, tiles):
        win = pl.ds(row, rows)
        mid = [[ref[t, p + i - 1, win, :] for i in range(count + 2)] for t in range(tiles)]
        mid += [[None] + [ref[t, p + i, win, :] for i in range(count)] for t in range(tiles, self.tiles)]
        found = []
        for i in range(count):
            left, right = self.beside([mid[t][i + 1] for t in range(self.tiles)])
            for t in range(tiles):
                near = [
                    mid[t][i + 2],
                    mid[t][i],
                    ref[t, p + i, pl.ds(row + 1, rows), :],
                    ref[t, p + i, pl.ds(row - 1, rows), :],
                    left[t],
                    right[t],
                ]
                found.append((t, p + i, mid[t][i + 1], near))
        return found

    def coefficients(self, kappa, sigma, coef, low, high, size, row, rows, chunk, finish):
        def block(first, count):
            for start_row in range(row, row + rows, chunk):
                win = pl.ds(start_row, chunk)
                n = lane(chunk)
                for t, p, k, near in self.around(kappa, first, count, start_row, chunk, self.tiles):
                    if self.closed:
                        near[4] = jnp.where(n == 0, 0.0, near[4])
                        near[5] = jnp.where(n == 127, 0.0, near[5])
                    face = [(0.5 * self.scale) * (k + j) for j in near]
                    diag = (face[0] + face[1]) + (face[2] + face[3]) + (face[4] + face[5])
                    diag = diag + sigma[t, p, win, :]
                    inverse = jnp.where(k > 0.0, 1.0 / diag, 0.0)
                    if self.closed:
                        face[4] = jnp.where(n == 0, 0.0, face[4])
                        face[5] = jnp.where(n == 127, 0.0, face[5])
                    for j in range(6):
                        coef[j, t, p, win, :] = face[j] * inverse
                    finish(t, p, start_row, chunk, diag, inverse)

        groups(low, high, size, block)

    def defects(self, x, rhs, coef, low, high, size, row, rows, chunk, tiles, use):
        def block(first, count):
            for start_row in range(row, row + rows, chunk):
                win = pl.ds(start_row, chunk)
                found = []
                for t, p, mid, near in self.around(x, first, count, start_row, chunk, tiles):
                    c = [coef[j, t, p, win, :] for j in range(6)]
                    a = (c[0] * near[0] + c[1] * near[1]) + (c[2] * near[2] + c[3] * near[3])
                    b = (rhs[t, p, win, :] - mid) + (c[4] * near[4] + c[5] * near[5])
                    found.append((t, p, mid, a + b))
                for t, p, mid, value in found:
                    use(t, p, start_row, chunk, mid, value)

        groups(low, high, size, block)

    def sweep(self, src, dst, rhs, coef, weight, low, high, size, row, rows, chunk):
        def use(t, p, r, n, mid, value):
            dst[t, p, pl.ds(r, n), :] = mid + weight * value

        self.defects(src, rhs, coef, low, high, size, row, rows, chunk, self.tiles, use)

    def residual(self, x, rhs, coef, diag, dst, low, high, size, row, rows, chunk):
        def use(t, p, r, n, mid, value):
            dst[0, p, pl.ds(r, n), :] = diag[0, p, pl.ds(r, n), :] * value

        self.defects(x, rhs, coef, low, high, size, row, rows, chunk, 1, use)


def restrict(load, planes, matrix, store):
    sums = [
        load(2 * i, 0) + load(2 * i, 1) + load(2 * i + 1, 0) + load(2 * i + 1, 1)
        for i in range(planes)
    ]
    rows = sums[0].shape[0]
    out = product(jnp.concatenate(sums, axis=0), matrix)
    for i in range(planes):
        store(i, out[i * rows : (i + 1) * rows, :])


def kernel(rhs, kappa, sigma, out, s):
    gx, gy, gz = lax.axis_index("gx"), lax.axis_index("gy"), lax.axis_index("gz")
    nx, ny, nz = 4, 4, 8
    links = Links(s["send"], s["recv"])
    s = dict(s)
    for level in "123":
        s["K" + level] = s["KS" + level].at[pl.ds(0, 1)]
        s["S" + level] = s["KS" + level].at[pl.ds(1, 1)]
    has = {
        ("x", 1): gx < nx - 1,
        ("x", -1): gx > 0,
        ("y", 1): gy < ny - 1,
        ("y", -1): gy > 0,
        ("z", 1): gz < nz - 1,
        ("z", -1): gz > 0,
        ("x", 0): None,
        ("y", 0): None,
    }

    def clear(ref, *index):
        part = ref.at[index] if index else ref
        part[...] = jnp.zeros(part.shape, F32)

    def clear_edges(ref, planes, rows):
        total = ref.shape[1]
        pl.when(gx == 0)(lambda: clear(ref, 0, pl.ds(0, planes[0])))
        pl.when(gx == nx - 1)(lambda: clear(ref, 0, pl.ds(planes[1], total - planes[1])))
        pl.when(gy == 0)(lambda: clear(ref, 0, slice(None), pl.ds(rows[0], rows[1])))
        pl.when(gy == ny - 1)(lambda: clear(ref, 0, slice(None), pl.ds(rows[2], rows[1])))

    for name in ("K0", "S0", "B0", "N0"):
        clear_edges(s[name], (7, 23), (8, 8, 80))
    for name in ("K1", "S1", "B1", "N1", "E1"):
        clear_edges(s[name], (8, 16), (8, 8, 48))
    every = slice(None)
    pl.when(gy == 0)(lambda: clear(s["Q2"], every, every, every, pl.ds(0, 16)))
    pl.when(gy == ny - 1)(lambda: clear(s["Q2"], every, every, every, pl.ds(32, 16)))
    for name in ("K2", "XA2", "XB2"):
        clear(s[name], 0, 0)
        clear(s[name], 0, 17)
    for name, planes, rows in (("3", 8, 32), ("4", 4, 16)):
        for field in ("K", "XA", "XB"):
            ref = s[field + name]
            clear(ref, 0, 0)
            clear(ref, 0, planes + 1)
            clear(ref, 0, slice(None), pl.ds(0, 8))
            clear(ref, 0, slice(None), pl.ds(8 + rows, 8))
    for name in ("G0", "GN0"):
        clear(s[name])

    @pl.when((gz == 0) | (gz == nz - 1))
    def _():
        for name in ("Z0", "ZN0", "Z1", "Z2"):
            clear(s[name])

    barrier = pltpu.get_barrier_semaphore()
    plane_mates = [
        (lax.rem(gx + i, nx), lax.rem(gy + j, ny), gz)
        for i in range(nx)
        for j in range(ny)
        if i or j
    ]
    line_mates = [(gx, gy, lax.rem(gz + i, nz)) for i in range(1, nz)]
    for mate in plane_mates + line_mates:
        pl.semaphore_signal(barrier, inc=1, device_id=mate, device_id_type=MESH)

    around = [(dx, dy) for dx in (1, -1, 0) for dy in (0, 1, -1) if dx or dy]

    def neighbours(make, first=None):
        copies = []
        for m, (dx, dy) in enumerate(around):
            src, dst = make(dx, dy)
            copies.append(
                links.copy(
                    src,
                    dst,
                    (gx + dx, gy + dy, gz),
                    both(has["x", dx], has["y", dy]),
                    both(has["x", -dx], has["y", -dy]),
                    None if first is None else first + m,
                )
            )
        return copies

    def sides(src, slots):
        return [
            links.copy(src, slots.at[0], (gx, gy, gz + 1), has["z", 1], has["z", -1]),
            links.copy(src, slots.at[1], (gx, gy, gz - 1), has["z", -1], has["z", 1]),
        ]

    def main0(src, first, ref, h, k=None):
        def make(dx, dy):
            sp = {1: (first + 16 - h, h), -1: (first, h), 0: (first, 16)}[dx]
            dp = {1: (7 - h, h), -1: (23, h), 0: (7, 16)}[dx]
            sr = {1: (56, 8), -1: (0, 8), 0: (0, 64)}[dy]
            dr = {1: (8, 8), -1: (80, 8), 0: (16, 64)}[dy]
            base = 0 if src is not ref else 16
            source = src.at[pl.ds(*sp), pl.ds(base + sr[0], sr[1])] if base == 0 else src.at[
                0, pl.ds(*sp), pl.ds(base + sr[0], sr[1])
            ]
            return source, ref.at[0, pl.ds(*dp), pl.ds(*dr)]

        return neighbours(make, k)

    inner = [
        pltpu.make_async_copy(src, s[name].at[0, pl.ds(7, 16), pl.ds(16, 64)], s["local"].at[k])
        for k, (src, name) in enumerate(((kappa, "K0"), (sigma, "S0"), (rhs, "B0")))
    ]
    for made in inner:
        made.start()
    mains = main0(kappa, 0, s["K0"], 7) + main0(sigma, 0, s["S0"], 6)
    main_b = main0(rhs, 0, s["B0"], 6)
    for made in inner:
        made.wait()

    def pack0(load, dst):
        n = lane(64)
        for g in range(2):
            total = jnp.zeros((64, 128), F32)
            for q in range(8):
                moved = turn(load(8 * g + q), 16 * q + 8)
                total = jnp.where((n >= 16 * q) & (n < 16 * q + 16), moved, total)
            dst[g, :, :] = total

    for a, name in enumerate(("K0", "S0", "B0")):
        pack0(lambda i, ref=s[name]: ref[0, 7 + i, 16:80, :], s["P0"].at[a])
    side0 = sides(s["P0"], s["Z0"])
    pl.semaphore_wait(barrier, len(plane_mates + line_mates))
    start(mains)
    start(side0)

    to1 = halving(0, 32, 64)
    to2 = halving(32, 48, 32)
    to3 = halving(48, 16 * gz, 16)
    to4 = halving(0, 0, 64)
    own2 = pl.ds(1 + 4 * gx, 4)
    own3 = pl.ds(1 + 2 * gx, 2)
    row3 = pl.ds(pl.multiple_of(8 + 8 * gy, 8), 8)

    def down1(src, first, row, dst):
        def store(i, v):
            dst[0, 8 + i, 16:48, :] = v

        restrict(lambda i, o: src[0, first + i, pl.ds(row + o, 32, stride=2), :], 8, to1, store)

    def down2(src, dst):
        def store(i, v):
            dst[0, 1 + 4 * gx + i, 24:40, :] = v

        restrict(lambda i, o: src[0, 8 + i, pl.ds(16 + o, 16, stride=2), :], 4, to2, store)

    def down3(src, use):
        def store(i, v):
            s["Z3"][gz, use, i, :, :] = v

        restrict(
            lambda i, o: src[0, 1 + 4 * gx + i, pl.ds(24 + o, 8, stride=2), :], 2, to3, store
        )

    def down4(src, dst):
        def store(i, v):
            dst[0, 1 + i, 8:24, :] = v

        restrict(lambda i, o: src[0, 1 + i, pl.ds(8 + o, 16, stride=2), :], 4, to4, store)

    def pack1(ref, use):
        n = lane(32)
        total = jnp.zeros((32, 128), F32)
        for q in range(8):
            v = ref[0, 8 + q, 16:48, :]
            v = turn(v + turn(v, 64), 16 * q - 24)
            total = jnp.where((n >= 16 * q) & (n < 16 * q + 16), v, total)
        s["P1"][use, :, :] = total

    def side1(use, count=1):
        part = pl.ds(use, count)
        return sides(s["P1"].at[part], s["Z1"].at[:, part])

    def merge1(ref, use):
        n = lane(32)
        ghosts = jnp.where((n % 16) < 8, s["Z1"][0, use], s["Z1"][1, use])
        for q in range(8):
            low = turn(ghosts, 24 - 16 * q)
            high = turn(ghosts, 24 - 16 * q + 64)
            v = ref[0, 8 + q, 16:48, :]
            v = jnp.where((n >= 24) & (n < 32), low, v)
            ref[0, 8 + q, 16:48, :] = jnp.where((n >= 96) & (n < 104), high, v)

    def main1(ref, h, k=None):
        def make(dx, dy):
            sp = {1: (16 - h, h), -1: (8, h), 0: (8, 8)}[dx]
            dp = {1: (8 - h, h), -1: (16, h), 0: (8, 8)}[dx]
            sr = {1: (40, 8), -1: (16, 8), 0: (16, 32)}[dy]
            dr = {1: (8, 8), -1: (48, 8), 0: (16, 32)}[dy]
            return ref.at[:, pl.ds(*sp), pl.ds(*sr)], ref.at[:, pl.ds(*dp), pl.ds(*dr)]

        return neighbours(make, k)

    def side2(ref, use, count=1):
        return sides(ref.at[:, own2, pl.ds(24, 16)], s["Z2"].at[:, pl.ds(use, count)])

    def merge2(ref, use):
        n = lane(16)
        whole = [
            ref[0, 1 + 4 * gx + i, 24:40, :]
            + turn(s["Z2"][0, use, i], -32)
            + turn(s["Z2"][1, use, i], 32)
            for i in range(4)
        ]
        for i in range(2):
            s["Q2"][use, gx, i, 16:32, :] = jnp.where(
                n < 64, turn(whole[i], -32), turn(whole[i + 2], 32)
            )

    def main2(use, count=1, first=None):
        copies = []
        for i in range(nx):
            for dy in (0, 1, -1):
                if i == 0 and dy == 0:
                    continue
                dr = {1: (0, 16), -1: (32, 16), 0: (16, 16)}[dy]
                part = s["Q2"].at[pl.ds(use, count), gx]
                copies.append(
                    links.copy(
                        part.at[:, :, pl.ds(16, 16)],
                        part.at[:, :, pl.ds(*dr)],
                        (lax.rem(gx + i, nx), gy + dy, gz),
                        has["y", dy],
                        has["y", -dy],
                        None if first is None else first + len(copies),
                    )
                )
        return copies

    def spread2(use, ref):
        n = lane(48)
        inside = (n >= 32) & (n < 96)
        for g in range(nx):
            for i in range(2):
                v = s["Q2"][use, g, i]
                ref[0, 1 + 4 * g + i, 8:56, :] = jnp.where(inside, turn(v, 32), 0.0)
                ref[0, 3 + 4 * g + i, 8:56, :] = jnp.where(inside, turn(v, -32), 0.0)

    def side3(use, count=1):
        part = s["Z3"].at[gz, pl.ds(use, count)]
        return [links.copy(part, part, mate) for mate in line_mates]

    def merge3(ref, use):
        for i in range(2):
            total = s["Z3"][0, use, i]
            for q in range(1, nz):
                total = total + s["Z3"][q, use, i]
            ref[0, 1 + 2 * gx + i, row3, :] = total

    def main3(ref):
        part = ref.at[:, own3, row3]
        return [links.copy(part, part, mate) for mate in plane_mates]

    down1(s["K0"], 7, 16, s["K1"])
    down1(s["S0"], 7, 16, s["S1"])
    pack1(s["K1"], 0)
    pack1(s["S1"], 1)
    side_ks1 = side1(0, 2)
    start(side_ks1)
    down2(s["K1"], s["K2"])
    down2(s["S1"], s["S2"])
    side_ks2 = side2(s["KS2"], 0, 2)
    start(side_ks2)
    down3(s["K2"], 0)
    down3(s["S2"], 1)
    side_ks3 = side3(0, 2)
    start(side_ks3)

    wait(side0)
    n64 = lane(64)
    for a in range(3):
        for g in range(2):
            s["G0"][a, 1 + g, 8:72, :] = jnp.where(
                (n64 % 16) < 8, s["Z0"][0, a, g], s["Z0"][1, a, g]
            )

    def ghost0(ref, k=None):
        def make(dx, dy):
            sg = {1: (2, 1), -1: (1, 1), 0: (1, 2)}[dx]
            dg = {1: (0, 1), -1: (3, 1), 0: (1, 2)}[dx]
            sr = {1: (64, 8), -1: (8, 8), 0: (8, 64)}[dy]
            dr = {1: (0, 8), -1: (72, 8), 0: (8, 64)}[dy]
            return ref.at[:, pl.ds(*sg), pl.ds(*sr)], ref.at[:, pl.ds(*dg), pl.ds(*dr)]

        return neighbours(make, k)

    def unpack0(src, ref):
        n = lane(80)
        edge = (n < 8) | (n >= 120)

        for g in range(4):
            v = src[g]
            for q in range(8):
                p = 8 * g + q - 1
                if 0 <= p < 30:
                    ref[1, p, 8:88, :] = jnp.where(edge, turn(v, -16 * q - 8), 0.0)

    first_ghost = links.used
    ghosts = ghost0(s["G0"])
    start(ghosts)
    start(main_b)

    wait(side_ks1)
    merge1(s["K1"], 0)
    merge1(s["S1"], 1)
    main_ks1 = main1(s["KS1"], 7)
    wait(side_ks2)
    merge2(s["K2"], 0)
    merge2(s["S2"], 1)
    first_main2 = links.used
    main_ks2 = main2(0, 2)
    wait(side_ks3)
    merge3(s["K3"], 0)
    merge3(s["S3"], 1)
    main_ks3 = main3(s["KS3"])

    wait(ghosts)
    for a, name in enumerate(("K0", "S0", "B0")):
        unpack0(s["G0"].at[a], s[name])
    wait(mains)

    weights = cheb(SWEEPS)
    level0 = Level(2, 1.0)
    c0, b0, xa0, xb0 = s["C0"], s["B0"], s["S0"], s["XB0"]

    def finish0(t, p, r, n, diag, inverse):
        win = pl.ds(r, n)
        xa0[t, p, win, :] = inverse
        if t == 0:
            s["D0"][0, p, win, :] = diag

    def rows0(h):
        return (8, 80, 16) if h > 4 else (12, 72, 24) if h > 0 else (16, 64, 16)

    level0.coefficients(s["K0"], s["S0"], c0, 1, 29, 4, 8, 80, 16, finish0)
    wait(main_b)
    start(main_ks1)
    start(main_ks2)
    start(main_ks3)

    def begin0(first, count):
        for t in range(2):
            for i in range(count):
                part = (t, first + i, pl.ds(8, 80), slice(None))
                scaled = b0[part] * xa0[part]
                b0[part] = scaled
                xa0[part] = weights[0] * scaled

    groups(1, 29, 4, begin0)
    x, y = xa0, xb0
    for t in range(1, SWEEPS):
        h = 6 - t
        level0.sweep(x, y, b0, c0, weights[t], 7 - h, 23 + h, 8 + h, *rows0(h))
        x, y = y, x
    level0.residual(x, b0, c0, s["D0"], s["R0"], 7, 23, 8, *rows0(0))
    pre0 = x

    down1(s["R0"], 7, 16, s["B1"])
    pack1(s["B1"], 2)
    round1 = side1(2)
    start(round1)
    pack0(lambda i: pre0[0, 7 + i, 16:80, :], s["PN0"].at[0])
    side_n0 = sides(s["PN0"], s["ZN0"])
    start(side_n0)

    level1 = Level(1, 0.25)
    level2 = Level(1, 0.0625)
    level3 = Level(1, 0.015625, closed=True)
    level4 = Level(1, 0.00390625)
    all3, all4 = (1, 9, 8, 8, 32, 32), (1, 5, 4, 8, 16, 16)

    def part1(h):
        return (8 - h, 16 + h, 8 + 2 * h) + ((8, 48, 48) if h > 4 else (12, 40, 40))

    def part2(h):
        return (1, 17, 16) + ((16, 32, 32) if h > 4 else (20, 24, 24))

    def finish(name):
        def keep(t, p, r, n, diag, inverse):
            s["D" + name][t, p, pl.ds(r, n), :] = diag
            s["I" + name][t, p, pl.ds(r, n), :] = inverse

        return keep

    wait(main_ks1)
    level1.coefficients(s["K1"], s["S1"], s["C1"], 2, 22, 5, 8, 48, 48, finish("1"))
    wait(round1)
    merge1(s["B1"], 2)
    round1 = main1(s["B1"], 6)
    start(round1)

    for i in range(16):
        s["N0"][0, 7 + i, 16:80, :] = pre0[0, 7 + i, 16:80, :]
    main_n0 = main0(s["N0"], 7, s["N0"], 6, 0)
    wait(side_n0)
    for g in range(2):
        s["GN0"][0, 1 + g, 8:72, :] = jnp.where(
            (n64 % 16) < 8, s["ZN0"][0, 0, g], s["ZN0"][1, 0, g]
        )
    ghosts = ghost0(s["GN0"], first_ghost)
    wait(main_ks2)
    spread2(0, s["K2"])
    spread2(1, s["S2"])
    wait(main_ks3)
    down4(s["K3"], s["K4"])
    down4(s["S3"], s["S4"])
    level2.coefficients(s["K2"], s["S2"], s["C2"], 1, 17, 8, 16, 32, 32, finish("2"))
    level3.coefficients(s["K3"], s["S3"], s["C3"], *all3, finish("3"))
    level4.coefficients(s["K4"], s["S4"], s["C4"], *all4, finish("4"))

    def begin(name, low, high, size, row, rows, chunk):
        def block(first, count):
            for i in range(count):
                part = (0, first + i, pl.ds(row, rows), slice(None))
                scaled = s["B" + name][part] * s["I" + name][part]
                s["B" + name][part] = scaled
                s["XA" + name][part] = first_weight(name) * scaled

        groups(low, high, size, block)

    def first_weight(name):
        return cheb(BOTTOM_SWEEPS if name == "4" else SWEEPS)[0]

    wait(round1)
    start(ghosts)
    start(main_n0)
    begin("1", *part1(6))
    x, y = s["XA1"], s["XB1"]
    for t in range(1, SWEEPS):
        h = 6 - t
        level1.sweep(x, y, s["B1"], s["C1"], weights[t], *part1(h))
        x, y = y, x
    level1.residual(x, s["B1"], s["C1"], s["D1"], y, 8, 16, 8, 16, 32, 32)

    down2(y, s["B2"])
    round2 = side2(s["B2"], 2)
    start(round2)
    n32 = lane(32)
    for i in range(8):
        s["N1"][0, 8 + i, 16:48, :] = jnp.where(
            (n32 >= 32) & (n32 < 96), x[0, 8 + i, 16:48, :], 0.0
        )
    pack1(s["N1"], 3)
    side_n1 = side1(3)
    start(side_n1)
    wait(round2)
    merge2(s["B2"], 2)
    round2 = main2(2)
    start(round2)
    wait(side_n1)
    merge1(s["N1"], 3)
    main_n1 = main1(s["N1"], 6, 8)
    wait(round2)
    start(main_n1)
    spread2(2, s["B2"])
    begin("2", *part2(6))
    x, y = s["XA2"], s["XB2"]
    for t in range(1, SWEEPS):
        level2.sweep(x, y, s["B2"], s["C2"], weights[t], *part2(6 - t))
        x, y = y, x
    level2.residual(x, s["B2"], s["C2"], s["D2"], s["R2"], 1, 17, 16, 24, 16, 16)

    down3(s["R2"], 2)
    round3 = side3(2)
    start(round3)
    n16 = lane(16)
    for i in range(4):
        p = 1 + 4 * gx + i
        s["N2"][0, p, 24:40, :] = jnp.where((n16 >= 48) & (n16 < 80), x[0, p, 24:40, :], 0.0)
    side_n2 = side2(s["N2"], 3)
    start(side_n2)
    wait(round3)
    merge3(s["B3"], 2)
    round3 = main3(s["B3"])
    start(round3)
    wait(side_n2)
    merge2(s["N2"], 3)
    wait(round3)
    main_n2 = main2(3, 1, first_main2)
    start(main_n2)

    begin("3", *all3)
    x, y = s["XA3"], s["XB3"]
    for t in range(1, SWEEPS):
        level3.sweep(x, y, s["B3"], s["C3"], weights[t], *all3)
        x, y = y, x
    level3.residual(x, s["B3"], s["C3"], s["D3"], s["R3"], *all3)
    down4(s["R3"], s["B4"])

    begin("4", *all4)
    u, v = s["XA4"], s["XB4"]
    for weight in cheb(BOTTOM_SWEEPS)[1:]:
        level4.sweep(u, v, s["B4"], s["C4"], weight, *all4)
        u, v = v, u

    def spread(rows, planes, matrix, load, dst):
        value = product(jnp.concatenate([load(i) for i in range(planes)], axis=0), matrix)
        for i in range(planes):
            part = value[i * rows : (i + 1) * rows, :]
            dst[i, pl.ds(0, rows, stride=2), :] = part
            dst[i, pl.ds(1, rows, stride=2), :] = part

    fine = s["T"]
    spread(16, 4, doubling(0, 0, 0, 128), lambda i: u[0, 1 + i, 8:24, :], fine)
    for i in range(8):
        y[0, 1 + i, 8:40, :] = x[0, 1 + i, 8:40, :] + fine[i // 2, 0:32, :]
    for t in range(SWEEPS):
        x, y = y, x
        level3.sweep(x, y, s["B3"], s["C3"], weights[t], *all3)
    e3 = y

    wait(main_n2)
    spread2(3, s["N2"])
    rows3 = pl.ds(pl.multiple_of(8 * gy, 8), 24)
    spread(24, 8, doubling(16 * gz, 48, 16, 112), lambda i: e3[0, 1 + i, rows3, :], fine)
    y, x = s["XA2"], s["XB2"]
    for i in range(16):
        y[0, 1 + i, 12:52, :] = s["N2"][0, 1 + i, 12:52, :] + fine[i // 2, 4:44, :]
    for t in range(SWEEPS):
        x, y = y, x
        level2.sweep(x, y, s["B2"], s["C2"], weights[t], *part2(8 - t))
    e2 = y

    wait(main_n1)
    value = product(
        jnp.concatenate([e2[0, 1 + i, 20:44, :] for i in range(16)], axis=0),
        doubling(48, 32, 24, 104),
    )
    fine1 = s["T1"]
    pl.when(gx == 0)(lambda: clear(fine1, pl.ds(0, 4)))
    pl.when(gx == nx - 1)(lambda: clear(fine1, pl.ds(20, 4)))
    for i in range(16):
        part = value[i * 24 : (i + 1) * 24, :]
        fine1[4 + i, pl.ds(0, 24, stride=2), :] = part
        fine1[4 + i, pl.ds(1, 24, stride=2), :] = part
    y, x = s["XA1"], s["XB1"]
    for p in range(-6, 14):
        y[0, 8 + p, 8:56, :] = s["N1"][0, 8 + p, 8:56, :] + fine1[4 + 4 * gx + p // 2, 0:48, :]
    for t in range(SWEEPS):
        x, y = y, x
        h = 5 - t
        level1.sweep(x, y, s["B1"], s["C1"], weights[t], *part1(h))
    for i in range(8):
        s["E1"][0, 8 + i, 16:48, :] = jnp.where(
            (n32 >= 32) & (n32 < 96), y[0, 8 + i, 16:48, :], 0.0
        )
    pack1(s["E1"], 4)
    round1 = side1(4)
    start(round1)
    wait(ghosts)
    unpack0(s["GN0"].at[0], s["N0"])
    wait(round1)
    merge1(s["E1"], 4)
    round1 = main1(s["E1"], 3, 16)
    start(round1)
    wait(main_n0)
    wait(round1)

    to_main = doubling(32, 0, 0, 128)
    to_side = doubling(32, -128, 0, 8) + doubling(32, 128, 120, 128)
    xa0 = s["S0"]
    for i in range(14):
        e = s["E1"][0, 5 + i, 12:52, :]
        for t, matrix in ((0, to_main), (1, to_side)):
            part = product(e, matrix)
            s["T0"][t, pl.ds(0, 40, stride=2), :] = part
            s["T0"][t, pl.ds(1, 40, stride=2), :] = part
            for o in range(2):
                p = 1 + 2 * i + o
                xa0[t, p, 8:88, :] = s["N0"][t, p, 8:88, :] + s["T0"][t, 0:80, :]
    x, y = s["XB0"], xa0
    for t in range(SWEEPS - 1):
        x, y = y, x
        h = 5 - t
        level0.sweep(x, y, b0, c0, weights[t], 7 - h, 23 + h, 8 + h, *rows0(h))

    def last(t, p, r, n, mid, value):
        out[p - 7, pl.ds(r - 16, n), :] = mid + weights[SWEEPS - 1] * value

    level0.defects(y, b0, c0, 7, 23, 8, *rows0(0), 1, last)


def scratch():
    shapes = {}
    for name in ("K0", "S0", "B0", "N0", "XB0"):
        shapes[name] = (2, 30, 96, 128)
    shapes["C0"] = (6, 2, 30, 96, 128)
    shapes["D0"], shapes["R0"] = (1, 30, 96, 128), (1, 23, 88, 128)
    shapes["P0"], shapes["Z0"], shapes["G0"] = (3, 2, 64, 128), (2, 3, 2, 64, 128), (3, 4, 80, 128)
    shapes["PN0"], shapes["ZN0"] = (1, 2, 64, 128), (2, 1, 2, 64, 128)
    shapes["GN0"] = (1, 4, 80, 128)
    shapes["T0"] = (2, 88, 128)
    for level, dims in (("1", (24, 64, 128)), ("2", (18, 64, 128)), ("3", (10, 48, 128)), ("4", (6, 32, 128))):
        for name in ("K", "S", "B", "I", "D", "XA", "XB"):
            shapes[name + level] = (1,) + dims
        if level != "4":
            del shapes["K" + level], shapes["S" + level]
            shapes["KS" + level] = (2,) + dims
        shapes["C" + level] = (6, 1) + dims
    shapes["N1"] = shapes["E1"] = shapes["B1"]
    shapes["N2"] = shapes["R2"] = shapes["B2"]
    shapes["R3"] = shapes["B3"]
    shapes["P1"], shapes["Z1"] = (5, 32, 128), (2, 5, 32, 128)
    shapes["Z2"], shapes["Q2"] = (2, 4, 4, 16, 128), (4, 4, 2, 48, 128)
    shapes["Z3"] = (8, 3, 2, 8, 128)
    shapes["T"], shapes["T1"] = (8, 56, 128), (24, 56, 128)
    return {
        "send": pltpu.SemaphoreType.DMA((COPIES,)),
        "recv": pltpu.SemaphoreType.DMA((COPIES,)),
        "local": pltpu.SemaphoreType.DMA((3,)),
        **{name: pltpu.VMEM(shape, F32) for name, shape in shapes.items()},
    }


def on_device(rhs, kappa, sigma):
    return pl.pallas_call(
        kernel,
        out_shape=jax.ShapeDtypeStruct(rhs.shape, F32),
        in_specs=[pl.BlockSpec(memory_space=pl.ANY)] * 3,
        out_specs=pl.BlockSpec(memory_space=pltpu.VMEM),
        scratch_shapes=[scratch()],
        compiler_params=pltpu.CompilerParams(
            collective_id=0, has_side_effects=True, vmem_limit_bytes=63 * 2**20
        ),
    )(rhs, kappa, sigma)


def solution(mesh):
    placed = (P("gx", "gy", "gz"), P("gx", "gy", "gz"), P("gx", "gy", "gz"))
    return jax.shard_map(
        on_device, mesh=mesh, in_specs=placed, out_specs=P("gx", "gy", "gz"), check_vma=False
    )
```

```python
from functools import partial
import math

import jax
import jax.numpy as jnp
from jax import lax
from jax.experimental import pallas as pl
from jax.experimental.pallas import tpu as pltpu
from jax.sharding import PartitionSpec as P

LEVELS = 4
SWEEPS = 6
BOTTOM_SWEEPS = 8
MESH = pl.DeviceIdType.MESH
F32 = jnp.float32
COPIES = 132


def cheb(count):
    return [
        1.0 / (1.125 + 0.875 * math.cos(math.pi * (2 * t + 1) / (2 * count))) for t in range(count)
    ]


def lane(rows):
    return lax.broadcasted_iota(jnp.int32, (rows, 128), 1)


def turn(value, shift):
    shift = shift % 128
    return value if shift == 0 else pltpu.roll(value, shift, 1)


def product(value, matrix):
    return jnp.dot(value, matrix, precision=lax.Precision.HIGHEST, preferred_element_type=F32)


def halving(fine0, coarse0, count):
    i = lax.broadcasted_iota(jnp.int32, (128, 128), 0)
    j = lax.broadcasted_iota(jnp.int32, (128, 128), 1)
    offset = (i - fine0) - 2 * (j - coarse0)
    good = ((offset == 0) | (offset == 1)) & (j >= coarse0) & (j < coarse0 + count)
    return jnp.where(good, 0.125, 0.0).astype(F32)


def doubling(coarse0, fine0, low, high):
    i = lax.broadcasted_iota(jnp.int32, (128, 128), 0)
    j = lax.broadcasted_iota(jnp.int32, (128, 128), 1)
    offset = (j - fine0) - 2 * (i - coarse0)
    good = ((offset == 0) | (offset == 1)) & (j >= low) & (j < high)
    return jnp.where(good, 1.0, 0.0).astype(F32)


class Links:
    def __init__(self, send, recv):
        self.send, self.recv, self.used = send, recv, 0

    def copy(self, src, dst, target, send_ok=None, recv_ok=None, k=None):
        if k is None:
            k = self.used
            self.used += 1
        made = pltpu.make_async_remote_copy(
            src_ref=src,
            dst_ref=dst,
            send_sem=self.send.at[k],
            recv_sem=self.recv.at[k],
            device_id=target,
            device_id_type=MESH,
        )
        return made, send_ok, recv_ok


def given(flag, action):
    if flag is None:
        action()
    else:
        pl.when(flag)(action)


def start(copies):
    for made, send_ok, _ in copies:
        given(send_ok, made.start)


def wait(copies):
    for made, _, recv_ok in copies:
        given(recv_ok, made.wait_recv)
    for made, send_ok, _ in copies:
        given(send_ok, made.wait_send)


def both(a, b):
    if a is None:
        return b
    return a if b is None else a & b


def groups(low, high, size, action):
    whole = (high - low) // size
    if whole == 1:
        action(low, size)
    elif whole:

        def body(i, carry):
            action(low + size * i, size)
            return carry

        lax.fori_loop(0, whole, body, 0)
    rest = (high - low) % size
    if rest:
        action(high - rest, rest)


class Level:
    def __init__(self, tiles, scale, closed=False):
        self.tiles, self.scale, self.closed = tiles, scale, closed

    def beside(self, values):
        n = lane(values[0].shape[0])
        left = [turn(v, 1) for v in values]
        right = [turn(v, -1) for v in values]
        if self.tiles == 2:
            left = [jnp.where(n == 0, left[1 - t], left[t]) for t in range(2)]
            right = [jnp.where(n == 127, right[1 - t], right[t]) for t in range(2)]
        return left, right

    def around(self, ref, p, count, row, rows, tiles):
        win = pl.ds(row, rows)
        mid = [[ref[t, p + i - 1, win, :] for i in range(count + 2)] for t in range(tiles)]
        mid += [[None] + [ref[t, p + i, win, :] for i in range(count)] for t in range(tiles, self.tiles)]
        found = []
        for i in range(count):
            left, right = self.beside([mid[t][i + 1] for t in range(self.tiles)])
            for t in range(tiles):
                near = [
                    mid[t][i + 2],
                    mid[t][i],
                    ref[t, p + i, pl.ds(row + 1, rows), :],
                    ref[t, p + i, pl.ds(row - 1, rows), :],
                    left[t],
                    right[t],
                ]
                found.append((t, p + i, mid[t][i + 1], near))
        return found

    def coefficients(self, kappa, sigma, coef, low, high, size, row, rows, chunk, finish):
        def block(first, count):
            for start_row in range(row, row + rows, chunk):
                win = pl.ds(start_row, chunk)
                n = lane(chunk)
                for t, p, k, near in self.around(kappa, first, count, start_row, chunk, self.tiles):
                    if self.closed:
                        near[4] = jnp.where(n == 0, 0.0, near[4])
                        near[5] = jnp.where(n == 127, 0.0, near[5])
                    face = [(0.5 * self.scale) * (k + j) for j in near]
                    diag = (face[0] + face[1]) + (face[2] + face[3]) + (face[4] + face[5])
                    diag = diag + sigma[t, p, win, :]
                    inverse = jnp.where(k > 0.0, 1.0 / diag, 0.0)
                    if self.closed:
                        face[4] = jnp.where(n == 0, 0.0, face[4])
                        face[5] = jnp.where(n == 127, 0.0, face[5])
                    for j in range(6):
                        coef[j, t, p, win, :] = face[j] * inverse
                    finish(t, p, start_row, chunk, diag, inverse)

        groups(low, high, size, block)

    def defects(self, x, rhs, coef, low, high, size, row, rows, chunk, tiles, use):
        def block(first, count):
            for start_row in range(row, row + rows, chunk):
                win = pl.ds(start_row, chunk)
                found = []
                for t, p, mid, near in self.around(x, first, count, start_row, chunk, tiles):
                    c = [coef[j, t, p, win, :] for j in range(6)]
                    a = (c[0] * near[0] + c[1] * near[1]) + (c[2] * near[2] + c[3] * near[3])
                    b = (rhs[t, p, win, :] - mid) + (c[4] * near[4] + c[5] * near[5])
                    found.append((t, p, mid, a + b))
                for t, p, mid, value in found:
                    use(t, p, start_row, chunk, mid, value)

        groups(low, high, size, block)

    def sweep(self, src, dst, rhs, coef, weight, low, high, size, row, rows, chunk):
        def use(t, p, r, n, mid, value):
            dst[t, p, pl.ds(r, n), :] = mid + weight * value

        self.defects(src, rhs, coef, low, high, size, row, rows, chunk, self.tiles, use)

    def residual(self, x, rhs, coef, diag, dst, low, high, size, row, rows, chunk):
        def use(t, p, r, n, mid, value):
            dst[0, p, pl.ds(r, n), :] = diag[0, p, pl.ds(r, n), :] * value

        self.defects(x, rhs, coef, low, high, size, row, rows, chunk, 1, use)


def restrict(load, planes, matrix, store):
    sums = [
        load(2 * i, 0) + load(2 * i, 1) + load(2 * i + 1, 0) + load(2 * i + 1, 1)
        for i in range(planes)
    ]
    rows = sums[0].shape[0]
    out = product(jnp.concatenate(sums, axis=0), matrix)
    for i in range(planes):
        store(i, out[i * rows : (i + 1) * rows, :])


def kernel(rhs, kappa, sigma, out, s):
    gx, gy, gz = lax.axis_index("gx"), lax.axis_index("gy"), lax.axis_index("gz")
    nx, ny, nz = 4, 4, 8
    links = Links(s["send"], s["recv"])
    s = dict(s)
    for level in "123":
        s["K" + level] = s["KS" + level].at[pl.ds(0, 1)]
        s["S" + level] = s["KS" + level].at[pl.ds(1, 1)]
    has = {
        ("x", 1): gx < nx - 1,
        ("x", -1): gx > 0,
        ("y", 1): gy < ny - 1,
        ("y", -1): gy > 0,
        ("z", 1): gz < nz - 1,
        ("z", -1): gz > 0,
        ("x", 0): None,
        ("y", 0): None,
    }

    def clear(ref, *index):
        part = ref.at[index] if index else ref
        part[...] = jnp.zeros(part.shape, F32)

    def clear_edges(ref, planes, rows):
        total = ref.shape[1]
        pl.when(gx == 0)(lambda: clear(ref, 0, pl.ds(0, planes[0])))
        pl.when(gx == nx - 1)(lambda: clear(ref, 0, pl.ds(planes[1], total - planes[1])))
        pl.when(gy == 0)(lambda: clear(ref, 0, slice(None), pl.ds(rows[0], rows[1])))
        pl.when(gy == ny - 1)(lambda: clear(ref, 0, slice(None), pl.ds(rows[2], rows[1])))

    for name in ("K0", "S0", "B0", "N0"):
        clear_edges(s[name], (7, 23), (8, 8, 80))
    for name in ("K1", "S1", "B1", "N1", "E1"):
        clear_edges(s[name], (8, 16), (8, 8, 48))
    every = slice(None)
    pl.when(gy == 0)(lambda: clear(s["Q2"], every, every, every, pl.ds(0, 16)))
    pl.when(gy == ny - 1)(lambda: clear(s["Q2"], every, every, every, pl.ds(32, 16)))
    for name in ("K2", "XA2", "XB2"):
        clear(s[name], 0, 0)
        clear(s[name], 0, 17)
    for name, planes, rows in (("3", 8, 32), ("4", 4, 16)):
        for field in ("K", "XA", "XB"):
            ref = s[field + name]
            clear(ref, 0, 0)
            clear(ref, 0, planes + 1)
            clear(ref, 0, slice(None), pl.ds(0, 8))
            clear(ref, 0, slice(None), pl.ds(8 + rows, 8))
    for name in ("G0", "GN0"):
        clear(s[name])

    @pl.when((gz == 0) | (gz == nz - 1))
    def _():
        for name in ("Z0", "ZN0", "Z1", "Z2"):
            clear(s[name])

    barrier = pltpu.get_barrier_semaphore()
    plane_mates = [
        (lax.rem(gx + i, nx), lax.rem(gy + j, ny), gz)
        for i in range(nx)
        for j in range(ny)
        if i or j
    ]
    line_mates = [(gx, gy, lax.rem(gz + i, nz)) for i in range(1, nz)]
    for mate in plane_mates + line_mates:
        pl.semaphore_signal(barrier, inc=1, device_id=mate, device_id_type=MESH)

    around = [(dx, dy) for dx in (1, -1, 0) for dy in (0, 1, -1) if dx or dy]

    def neighbours(make, first=None):
        copies = []
        for m, (dx, dy) in enumerate(around):
            src, dst = make(dx, dy)
            copies.append(
                links.copy(
                    src,
                    dst,
                    (gx + dx, gy + dy, gz),
                    both(has["x", dx], has["y", dy]),
                    both(has["x", -dx], has["y", -dy]),
                    None if first is None else first + m,
                )
            )
        return copies

    def sides(src, slots):
        return [
            links.copy(src, slots.at[0], (gx, gy, gz + 1), has["z", 1], has["z", -1]),
            links.copy(src, slots.at[1], (gx, gy, gz - 1), has["z", -1], has["z", 1]),
        ]

    def main0(src, first, ref, h, k=None):
        def make(dx, dy):
            sp = {1: (first + 16 - h, h), -1: (first, h), 0: (first, 16)}[dx]
            dp = {1: (7 - h, h), -1: (23, h), 0: (7, 16)}[dx]
            sr = {1: (56, 8), -1: (0, 8), 0: (0, 64)}[dy]
            dr = {1: (8, 8), -1: (80, 8), 0: (16, 64)}[dy]
            base = 0 if src is not ref else 16
            source = src.at[pl.ds(*sp), pl.ds(base + sr[0], sr[1])] if base == 0 else src.at[
                0, pl.ds(*sp), pl.ds(base + sr[0], sr[1])
            ]
            return source, ref.at[0, pl.ds(*dp), pl.ds(*dr)]

        return neighbours(make, k)

    inner = [
        pltpu.make_async_copy(src, s[name].at[0, pl.ds(7, 16), pl.ds(16, 64)], s["local"].at[k])
        for k, (src, name) in enumerate(((kappa, "K0"), (sigma, "S0"), (rhs, "B0")))
    ]
    for made in inner:
        made.start()
    mains = main0(kappa, 0, s["K0"], 7) + main0(sigma, 0, s["S0"], 6)
    main_b = main0(rhs, 0, s["B0"], 6)
    for made in inner:
        made.wait()

    def pack0(load, dst):
        n = lane(64)
        for g in range(2):
            total = jnp.zeros((64, 128), F32)
            for q in range(8):
                moved = turn(load(8 * g + q), 16 * q + 8)
                total = jnp.where((n >= 16 * q) & (n < 16 * q + 16), moved, total)
            dst[g, :, :] = total

    for a, name in enumerate(("K0", "S0", "B0")):
        pack0(lambda i, ref=s[name]: ref[0, 7 + i, 16:80, :], s["P0"].at[a])
    side0 = sides(s["P0"], s["Z0"])
    pl.semaphore_wait(barrier, len(plane_mates + line_mates))
    start(mains)
    start(side0)

    to1 = halving(0, 32, 64)
    to2 = halving(32, 48, 32)
    to3 = halving(48, 16 * gz, 16)
    to4 = halving(0, 0, 64)
    own2 = pl.ds(1 + 4 * gx, 4)
    own3 = pl.ds(1 + 2 * gx, 2)
    row3 = pl.ds(pl.multiple_of(8 + 8 * gy, 8), 8)

    def down1(src, first, row, dst):
        def store(i, v):
            dst[0, 8 + i, 16:48, :] = v

        restrict(lambda i, o: src[0, first + i, pl.ds(row + o, 32, stride=2), :], 8, to1, store)

    def down2(src, dst):
        def store(i, v):
            dst[0, 1 + 4 * gx + i, 24:40, :] = v

        restrict(lambda i, o: src[0, 8 + i, pl.ds(16 + o, 16, stride=2), :], 4, to2, store)

    def down3(src, use):
        def store(i, v):
            s["Z3"][gz, use, i, :, :] = v

        restrict(
            lambda i, o: src[0, 1 + 4 * gx + i, pl.ds(24 + o, 8, stride=2), :], 2, to3, store
        )

    def down4(src, dst):
        def store(i, v):
            dst[0, 1 + i, 8:24, :] = v

        restrict(lambda i, o: src[0, 1 + i, pl.ds(8 + o, 16, stride=2), :], 4, to4, store)

    def pack1(ref, use):
        n = lane(32)
        total = jnp.zeros((32, 128), F32)
        for q in range(8):
            v = ref[0, 8 + q, 16:48, :]
            v = turn(v + turn(v, 64), 16 * q - 24)
            total = jnp.where((n >= 16 * q) & (n < 16 * q + 16), v, total)
        s["P1"][use, :, :] = total

    def side1(use, count=1):
        part = pl.ds(use, count)
        return sides(s["P1"].at[part], s["Z1"].at[:, part])

    def merge1(ref, use):
        n = lane(32)
        ghosts = jnp.where((n % 16) < 8, s["Z1"][0, use], s["Z1"][1, use])
        for q in range(8):
            low = turn(ghosts, 24 - 16 * q)
            high = turn(ghosts, 24 - 16 * q + 64)
            v = ref[0, 8 + q, 16:48, :]
            v = jnp.where((n >= 24) & (n < 32), low, v)
            ref[0, 8 + q, 16:48, :] = jnp.where((n >= 96) & (n < 104), high, v)

    def main1(ref, h, k=None):
        def make(dx, dy):
            sp = {1: (16 - h, h), -1: (8, h), 0: (8, 8)}[dx]
            dp = {1: (8 - h, h), -1: (16, h), 0: (8, 8)}[dx]
            sr = {1: (40, 8), -1: (16, 8), 0: (16, 32)}[dy]
            dr = {1: (8, 8), -1: (48, 8), 0: (16, 32)}[dy]
            return ref.at[:, pl.ds(*sp), pl.ds(*sr)], ref.at[:, pl.ds(*dp), pl.ds(*dr)]

        return neighbours(make, k)

    def side2(ref, use, count=1):
        return sides(ref.at[:, own2, pl.ds(24, 16)], s["Z2"].at[:, pl.ds(use, count)])

    def merge2(ref, use):
        n = lane(16)
        whole = [
            ref[0, 1 + 4 * gx + i, 24:40, :]
            + turn(s["Z2"][0, use, i], -32)
            + turn(s["Z2"][1, use, i], 32)
            for i in range(4)
        ]
        for i in range(2):
            s["Q2"][use, gx, i, 16:32, :] = jnp.where(
                n < 64, turn(whole[i], -32), turn(whole[i + 2], 32)
            )

    def main2(use, count=1, first=None):
        copies = []
        for i in range(nx):
            for dy in (0, 1, -1):
                if i == 0 and dy == 0:
                    continue
                dr = {1: (0, 16), -1: (32, 16), 0: (16, 16)}[dy]
                part = s["Q2"].at[pl.ds(use, count), gx]
                copies.append(
                    links.copy(
                        part.at[:, :, pl.ds(16, 16)],
                        part.at[:, :, pl.ds(*dr)],
                        (lax.rem(gx + i, nx), gy + dy, gz),
                        has["y", dy],
                        has["y", -dy],
                        None if first is None else first + len(copies),
                    )
                )
        return copies

    def spread2(use, ref):
        n = lane(48)
        inside = (n >= 32) & (n < 96)
        for g in range(nx):
            for i in range(2):
                v = s["Q2"][use, g, i]
                ref[0, 1 + 4 * g + i, 8:56, :] = jnp.where(inside, turn(v, 32), 0.0)
                ref[0, 3 + 4 * g + i, 8:56, :] = jnp.where(inside, turn(v, -32), 0.0)

    def side3(use, count=1):
        part = s["Z3"].at[gz, pl.ds(use, count)]
        return [links.copy(part, part, mate) for mate in line_mates]

    def merge3(ref, use):
        for i in range(2):
            total = s["Z3"][0, use, i]
            for q in range(1, nz):
                total = total + s["Z3"][q, use, i]
            ref[0, 1 + 2 * gx + i, row3, :] = total

    def main3(ref):
        part = ref.at[:, own3, row3]
        return [links.copy(part, part, mate) for mate in plane_mates]

    down1(s["K0"], 7, 16, s["K1"])
    down1(s["S0"], 7, 16, s["S1"])
    pack1(s["K1"], 0)
    pack1(s["S1"], 1)
    side_ks1 = side1(0, 2)
    start(side_ks1)
    down2(s["K1"], s["K2"])
    down2(s["S1"], s["S2"])
    side_ks2 = side2(s["KS2"], 0, 2)
    start(side_ks2)
    down3(s["K2"], 0)
    down3(s["S2"], 1)
    side_ks3 = side3(0, 2)
    start(side_ks3)

    wait(side0)
    n64 = lane(64)
    for a in range(3):
        for g in range(2):
            s["G0"][a, 1 + g, 8:72, :] = jnp.where(
                (n64 % 16) < 8, s["Z0"][0, a, g], s["Z0"][1, a, g]
            )

    def ghost0(ref, k=None):
        def make(dx, dy):
            sg = {1: (2, 1), -1: (1, 1), 0: (1, 2)}[dx]
            dg = {1: (0, 1), -1: (3, 1), 0: (1, 2)}[dx]
            sr = {1: (64, 8), -1: (8, 8), 0: (8, 64)}[dy]
            dr = {1: (0, 8), -1: (72, 8), 0: (8, 64)}[dy]
            return ref.at[:, pl.ds(*sg), pl.ds(*sr)], ref.at[:, pl.ds(*dg), pl.ds(*dr)]

        return neighbours(make, k)

    def unpack0(src, ref):
        n = lane(80)
        edge = (n < 8) | (n >= 120)

        for g in range(4):
            v = src[g]
            for q in range(8):
                p = 8 * g + q - 1
                if 0 <= p < 30:
                    ref[1, p, 8:88, :] = jnp.where(edge, turn(v, -16 * q - 8), 0.0)

    first_ghost = links.used
    ghosts = ghost0(s["G0"])
    start(ghosts)
    start(main_b)

    wait(side_ks1)
    merge1(s["K1"], 0)
    merge1(s["S1"], 1)
    main_ks1 = main1(s["KS1"], 7)
    wait(side_ks2)
    merge2(s["K2"], 0)
    merge2(s["S2"], 1)
    first_main2 = links.used
    main_ks2 = main2(0, 2)
    wait(side_ks3)
    merge3(s["K3"], 0)
    merge3(s["S3"], 1)
    main_ks3 = main3(s["KS3"])

    wait(ghosts)
    for a, name in enumerate(("K0", "S0", "B0")):
        unpack0(s["G0"].at[a], s[name])
    wait(mains)

    weights = cheb(SWEEPS)
    level0 = Level(2, 1.0)
    c0, b0, xa0, xb0 = s["C0"], s["B0"], s["S0"], s["XB0"]

    def finish0(t, p, r, n, diag, inverse):
        win = pl.ds(r, n)
        xa0[t, p, win, :] = inverse
        if t == 0:
            s["D0"][0, p, win, :] = diag

    def rows0(h):
        return (8, 80, 16) if h > 4 else (12, 72, 24) if h > 0 else (16, 64, 16)

    level0.coefficients(s["K0"], s["S0"], c0, 1, 29, 4, 8, 80, 16, finish0)
    wait(main_b)
    start(main_ks1)
    start(main_ks2)
    start(main_ks3)

    def begin0(first, count):
        for t in range(2):
            for i in range(count):
                part = (t, first + i, pl.ds(8, 80), slice(None))
                scaled = b0[part] * xa0[part]
                b0[part] = scaled
                xa0[part] = weights[0] * scaled

    groups(1, 29, 4, begin0)
    x, y = xa0, xb0
    for t in range(1, SWEEPS):
        h = 6 - t
        level0.sweep(x, y, b0, c0, weights[t], 7 - h, 23 + h, 8 + h, *rows0(h))
        x, y = y, x
    level0.residual(x, b0, c0, s["D0"], s["R0"], 7, 23, 8, *rows0(0))
    pre0 = x

    down1(s["R0"], 7, 16, s["B1"])
    pack1(s["B1"], 2)
    round1 = side1(2)
    start(round1)
    pack0(lambda i: pre0[0, 7 + i, 16:80, :], s["PN0"].at[0])
    side_n0 = sides(s["PN0"], s["ZN0"])
    start(side_n0)

    level1 = Level(1, 0.25)
    level2 = Level(1, 0.0625)
    level3 = Level(1, 0.015625, closed=True)
    level4 = Level(1, 0.00390625)
    all3, all4 = (1, 9, 8, 8, 32, 32), (1, 5, 4, 8, 16, 16)

    def part1(h):
        return (8 - h, 16 + h, 8 + 2 * h) + ((8, 48, 48) if h > 4 else (12, 40, 40))

    def part2(h):
        return (1, 17, 16) + ((16, 32, 32) if h > 4 else (20, 24, 24))

    def finish(name):
        def keep(t, p, r, n, diag, inverse):
            s["D" + name][t, p, pl.ds(r, n), :] = diag
            s["I" + name][t, p, pl.ds(r, n), :] = inverse

        return keep

    wait(main_ks1)
    level1.coefficients(s["K1"], s["S1"], s["C1"], 2, 22, 5, 8, 48, 48, finish("1"))
    wait(round1)
    merge1(s["B1"], 2)
    round1 = main1(s["B1"], 6)
    start(round1)

    for i in range(16):
        s["N0"][0, 7 + i, 16:80, :] = pre0[0, 7 + i, 16:80, :]
    main_n0 = main0(s["N0"], 7, s["N0"], 6, 0)
    wait(side_n0)
    for g in range(2):
        s["GN0"][0, 1 + g, 8:72, :] = jnp.where(
            (n64 % 16) < 8, s["ZN0"][0, 0, g], s["ZN0"][1, 0, g]
        )
    ghosts = ghost0(s["GN0"], first_ghost)
    wait(main_ks2)
    spread2(0, s["K2"])
    spread2(1, s["S2"])
    wait(main_ks3)
    down4(s["K3"], s["K4"])
    down4(s["S3"], s["S4"])
    level2.coefficients(s["K2"], s["S2"], s["C2"], 1, 17, 8, 16, 32, 32, finish("2"))
    level3.coefficients(s["K3"], s["S3"], s["C3"], *all3, finish("3"))
    level4.coefficients(s["K4"], s["S4"], s["C4"], *all4, finish("4"))

    def begin(name, low, high, size, row, rows, chunk):
        def block(first, count):
            for i in range(count):
                part = (0, first + i, pl.ds(row, rows), slice(None))
                scaled = s["B" + name][part] * s["I" + name][part]
                s["B" + name][part] = scaled
                s["XA" + name][part] = first_weight(name) * scaled

        groups(low, high, size, block)

    def first_weight(name):
        return cheb(BOTTOM_SWEEPS if name == "4" else SWEEPS)[0]

    wait(round1)
    start(ghosts)
    start(main_n0)
    begin("1", *part1(6))
    x, y = s["XA1"], s["XB1"]
    for t in range(1, SWEEPS):
        h = 6 - t
        level1.sweep(x, y, s["B1"], s["C1"], weights[t], *part1(h))
        x, y = y, x
    level1.residual(x, s["B1"], s["C1"], s["D1"], y, 8, 16, 8, 16, 32, 32)

    down2(y, s["B2"])
    round2 = side2(s["B2"], 2)
    start(round2)
    n32 = lane(32)
    for i in range(8):
        s["N1"][0, 8 + i, 16:48, :] = jnp.where(
            (n32 >= 32) & (n32 < 96), x[0, 8 + i, 16:48, :], 0.0
        )
    pack1(s["N1"], 3)
    side_n1 = side1(3)
    start(side_n1)
    wait(round2)
    merge2(s["B2"], 2)
    round2 = main2(2)
    start(round2)
    wait(side_n1)
    merge1(s["N1"], 3)
    main_n1 = main1(s["N1"], 6, 8)
    wait(round2)
    start(main_n1)
    spread2(2, s["B2"])
    begin("2", *part2(6))
    x, y = s["XA2"], s["XB2"]
    for t in range(1, SWEEPS):
        level2.sweep(x, y, s["B2"], s["C2"], weights[t], *part2(6 - t))
        x, y = y, x
    level2.residual(x, s["B2"], s["C2"], s["D2"], y, 1, 17, 16, 24, 16, 16)

    down3(y, 2)
    round3 = side3(2)
    start(round3)
    n16 = lane(16)
    for i in range(4):
        p = 1 + 4 * gx + i
        s["N2"][0, p, 24:40, :] = jnp.where((n16 >= 48) & (n16 < 80), x[0, p, 24:40, :], 0.0)
    side_n2 = side2(s["N2"], 3)
    start(side_n2)
    wait(round3)
    merge3(s["B3"], 2)
    round3 = main3(s["B3"])
    start(round3)
    wait(side_n2)
    merge2(s["N2"], 3)
    wait(round3)
    main_n2 = main2(3, 1, first_main2)
    start(main_n2)

    begin("3", *all3)
    x, y = s["XA3"], s["XB3"]
    for t in range(1, SWEEPS):
        level3.sweep(x, y, s["B3"], s["C3"], weights[t], *all3)
        x, y = y, x
    level3.residual(x, s["B3"], s["C3"], s["D3"], s["R3"], *all3)
    down4(s["R3"], s["B4"])

    begin("4", *all4)
    u, v = s["XA4"], s["XB4"]
    for weight in cheb(BOTTOM_SWEEPS)[1:]:
        level4.sweep(u, v, s["B4"], s["C4"], weight, *all4)
        u, v = v, u

    def spread(rows, planes, matrix, load, dst):
        value = product(jnp.concatenate([load(i) for i in range(planes)], axis=0), matrix)
        for i in range(planes):
            part = value[i * rows : (i + 1) * rows, :]
            dst[i, pl.ds(0, rows, stride=2), :] = part
            dst[i, pl.ds(1, rows, stride=2), :] = part

    fine = s["T"]
    spread(16, 4, doubling(0, 0, 0, 128), lambda i: u[0, 1 + i, 8:24, :], fine)
    for i in range(8):
        y[0, 1 + i, 8:40, :] = x[0, 1 + i, 8:40, :] + fine[i // 2, 0:32, :]
    for t in range(SWEEPS):
        x, y = y, x
        level3.sweep(x, y, s["B3"], s["C3"], weights[t], *all3)
    e3 = y

    wait(main_n2)
    spread2(3, s["N2"])
    rows3 = pl.ds(pl.multiple_of(8 * gy, 8), 24)
    spread(24, 8, doubling(16 * gz, 48, 16, 112), lambda i: e3[0, 1 + i, rows3, :], fine)
    y, x = s["XA2"], s["XB2"]
    for i in range(16):
        y[0, 1 + i, 12:52, :] = s["N2"][0, 1 + i, 12:52, :] + fine[i // 2, 4:44, :]
    for t in range(SWEEPS):
        x, y = y, x
        level2.sweep(x, y, s["B2"], s["C2"], weights[t], *part2(8 - t))
    e2 = y

    wait(main_n1)
    value = product(
        jnp.concatenate([e2[0, 1 + i, 20:44, :] for i in range(16)], axis=0),
        doubling(48, 32, 24, 104),
    )
    fine1 = s["T1"]
    pl.when(gx == 0)(lambda: clear(fine1, pl.ds(0, 4)))
    pl.when(gx == nx - 1)(lambda: clear(fine1, pl.ds(20, 4)))
    for i in range(16):
        part = value[i * 24 : (i + 1) * 24, :]
        fine1[4 + i, pl.ds(0, 24, stride=2), :] = part
        fine1[4 + i, pl.ds(1, 24, stride=2), :] = part
    y, x = s["XA1"], s["XB1"]
    for p in range(-6, 14):
        y[0, 8 + p, 8:56, :] = s["N1"][0, 8 + p, 8:56, :] + fine1[4 + 4 * gx + p // 2, 0:48, :]
    for t in range(SWEEPS):
        x, y = y, x
        h = 5 - t
        level1.sweep(x, y, s["B1"], s["C1"], weights[t], *part1(h))
    for i in range(8):
        s["E1"][0, 8 + i, 16:48, :] = jnp.where(
            (n32 >= 32) & (n32 < 96), y[0, 8 + i, 16:48, :], 0.0
        )
    pack1(s["E1"], 4)
    round1 = side1(4)
    start(round1)
    wait(ghosts)
    unpack0(s["GN0"].at[0], s["N0"])
    wait(round1)
    merge1(s["E1"], 4)
    round1 = main1(s["E1"], 3, 16)
    start(round1)
    wait(main_n0)
    wait(round1)

    to_main = doubling(32, 0, 0, 128)
    to_side = doubling(32, -128, 0, 8) + doubling(32, 128, 120, 128)
    xa0 = s["S0"]
    for first in (0, 7):
        coarse = jnp.concatenate([s["E1"][0, 5 + i, 12:52, :] for i in range(first, first + 7)], axis=0)
        for t, matrix in ((0, to_main), (1, to_side)):
            value = product(coarse, matrix)
            for i in range(7):
                part = value[40 * i : 40 * i + 40, :]
                s["T0"][t, i, pl.ds(0, 40, stride=2), :] = part
                s["T0"][t, i, pl.ds(1, 40, stride=2), :] = part
        for i in range(7):
            for t in range(2):
                for p in (1 + 2 * (first + i), 2 + 2 * (first + i)):
                    xa0[t, p, 8:88, :] = s["N0"][t, p, 8:88, :] + s["T0"][t, i, 0:80, :]
    x, y = s["XB0"], xa0
    for t in range(SWEEPS - 1):
        x, y = y, x
        h = 5 - t
        level0.sweep(x, y, b0, c0, weights[t], 7 - h, 23 + h, 8 + h, *rows0(h))

    def last(t, p, r, n, mid, value):
        out[p - 7, pl.ds(r - 16, n), :] = mid + weights[SWEEPS - 1] * value

    level0.defects(y, b0, c0, 7, 23, 8, *rows0(0), 1, last)


def scratch():
    shapes = {}
    for name in ("K0", "S0", "B0", "N0", "XB0"):
        shapes[name] = (2, 30, 96, 128)
    shapes["C0"] = (6, 2, 30, 96, 128)
    shapes["D0"], shapes["R0"] = (1, 30, 96, 128), (1, 23, 88, 128)
    shapes["P0"], shapes["Z0"], shapes["G0"] = (3, 2, 64, 128), (2, 3, 2, 64, 128), (3, 4, 80, 128)
    shapes["PN0"], shapes["ZN0"] = (1, 2, 64, 128), (2, 1, 2, 64, 128)
    shapes["GN0"] = (1, 4, 80, 128)
    shapes["T0"] = (2, 7, 88, 128)
    for level, dims in (("1", (24, 64, 128)), ("2", (18, 64, 128)), ("3", (10, 48, 128)), ("4", (6, 32, 128))):
        for name in ("K", "S", "B", "I", "D", "XA", "XB"):
            shapes[name + level] = (1,) + dims
        if level != "4":
            del shapes["K" + level], shapes["S" + level]
            shapes["KS" + level] = (2,) + dims
        shapes["C" + level] = (6, 1) + dims
    shapes["N1"] = shapes["E1"] = shapes["B1"]
    shapes["N2"] = shapes["B2"]
    shapes["R3"] = shapes["B3"]
    shapes["P1"], shapes["Z1"] = (5, 32, 128), (2, 5, 32, 128)
    shapes["Z2"], shapes["Q2"] = (2, 4, 4, 16, 128), (4, 4, 2, 48, 128)
    shapes["Z3"] = (8, 3, 2, 8, 128)
    shapes["T"], shapes["T1"] = (8, 56, 128), (24, 56, 128)
    return {
        "send": pltpu.SemaphoreType.DMA((COPIES,)),
        "recv": pltpu.SemaphoreType.DMA((COPIES,)),
        "local": pltpu.SemaphoreType.DMA((3,)),
        **{name: pltpu.VMEM(shape, F32) for name, shape in shapes.items()},
    }


def on_device(rhs, kappa, sigma):
    return pl.pallas_call(
        kernel,
        out_shape=jax.ShapeDtypeStruct(rhs.shape, F32),
        in_specs=[pl.BlockSpec(memory_space=pl.ANY)] * 3,
        out_specs=pl.BlockSpec(memory_space=pltpu.VMEM),
        scratch_shapes=[scratch()],
        compiler_params=pltpu.CompilerParams(
            collective_id=0, has_side_effects=True, vmem_limit_bytes=63 * 2**20
        ),
    )(rhs, kappa, sigma)


def solution(mesh):
    placed = (P("gx", "gy", "gz"), P("gx", "gy", "gz"), P("gx", "gy", "gz"))
    return jax.shard_map(
        on_device, mesh=mesh, in_specs=placed, out_specs=P("gx", "gy", "gz"), check_vma=False
    )
```
